256 devices in a mesh: layer: 2 (over core), row: 16 (over z, y_lo), col: 8 (over x, y_hi).
Axes of the slice: x: 4, y: 4 (y_hi: 2, y_lo: 2; y = y_hi * 2 + y_lo), z: 8, core: 2. Of those that a mesh axis runs over, the one named last changes fastest.
Arguments:
- left_tensor: float32 [2048, 8192], P('row', ('layer', 'col')), may hold values from -6 to 6
- right_tensor: float32 [8192, 8192], P(('layer', 'row'), 'col'), may hold values from -0.5 to 0.5
- left_occupied: int32 [32, 128], replicated, may hold values from 0 to 1, as said below
- right_occupied: int32 [128, 128], replicated, may hold values from 0 to 1, as said below
Outputs:
- polarizability: float32 [2048, 8192], P('row', 'col')
The draws below stay inside these ranges and needn't reach their ends.
Inputs may be any that keep to these rules, and one draw needn't show every extreme that they name: `left_occupied`: block occupancy flags. Each device's share of left_tensor (2 x 8 blocks) has at most 3 occupied blocks, and some share has exactly 3. `right_occupied`: block occupancy flags. Each device's share of right_tensor (4 x 16 blocks) has at most 12 occupied blocks, and some share has exactly 12.
All inputs are finite; a program needn't handle non-finite values.
Results may differ from the reference program's by a relative error of at most 0.000071.
Values sent between devices are 32-bit elements; how exact they have to be, the bound alone decides.
No kernel may reach another device: no remote copies, remote signals or barrier semaphores. Data moves between devices by JAX's collectives and lax.ppermute only.
A program may use at most 192 MiB of HBM per device.

```python
import jax
import jax.numpy as jnp
from jax import lax

BLK = 64
RB_DEV = 2
KB_SH = 8
CB_DEV = 16
RKB = 4
LCAP = 3
RCAP = 12
M = 2048
K = 8192
N = 8192
N_LAYER = 2
N_ROW = 16
N_COL = 8


def share_flags(key, group_rows, share_rows, group_cols, share_cols, most):
    shares = group_rows * group_cols
    size = share_rows * share_cols
    key_count, key_full, key_perm = jax.random.split(key, 3)
    counts = jax.random.randint(key_count, (shares,), most // 3, most + 1)
    fullest = jax.random.randint(key_full, (), 0, shares)
    counts = jnp.where(jnp.arange(shares) == fullest, most, counts)
    keys = jax.random.split(key_perm, shares)
    ranks = jax.vmap(lambda single: jax.random.permutation(single, size))(keys)
    flags = (ranks < counts[:, None]).astype(jnp.int32)
    flags = flags.reshape(group_rows, group_cols, share_rows, share_cols)
    flags = flags.transpose(0, 2, 1, 3)
    return flags.reshape(group_rows * share_rows, group_cols * share_cols)


def draw_left_occupied(key, part):
    key = jax.random.fold_in(key, 11)
    return share_flags(key, N_ROW, RB_DEV, N_LAYER * N_COL, KB_SH, LCAP)


def draw_right_occupied(key, part):
    key = jax.random.fold_in(key, 23)
    return share_flags(key, N_LAYER * N_ROW, RKB, N_COL, CB_DEV, RCAP)


def shard_levels(own_key, shape, cuts, least, top_value):
    level, own = 1.0, jax.random.fold_in(own_key, 6)
    for dim, parts in cuts:
        steps = jnp.exp(jax.random.uniform(jax.random.fold_in(own, dim), (parts,), jnp.float32, least / len(cuts), top_value / len(cuts)))
        level = level * jnp.repeat(steps, shape[dim] // parts).reshape([-1 if axis == dim else 1 for axis in range(len(shape))])
    return level


def scatter_about(own_key, extent, deviation, bound, shards=(), dtype=jnp.bfloat16):
    values = jax.random.normal(own_key, extent, jnp.float32) * deviation
    if len(shards) > 0:
        values = shard_levels(own_key, extent, shards, -0.22, 0.18) * values
    return jnp.clip(values, min=-bound, max=bound).astype(dtype)


def setup_inputs(seed: int = 0) -> dict:
    splits = jax.random.split(jax.random.key(seed), 5)
    return {
        "left_tensor": scatter_about(splits[0], (M, K), 1.0, 6.0, ((0, 16), (1, 16)), jnp.float32),
        "right_tensor": scatter_about(splits[1], (K, N), (2 * BLK) ** -0.5, 0.5, ((0, 32), (1, 8)), jnp.float32),
        "left_occupied": draw_left_occupied(jax.random.fold_in(splits[4], 71), 0),
        "right_occupied": draw_right_occupied(jax.random.fold_in(splits[4], 71), 0),
    }


def expand(occupied, size):
    flags = occupied.astype(jnp.float32)
    return jnp.repeat(jnp.repeat(flags, size, axis=0), size, axis=1)


def reference(left_tensor, right_tensor, left_occupied, right_occupied):
    left_sparse = left_tensor * expand(left_occupied, BLK)
    right_sparse = right_tensor * expand(right_occupied, BLK)
    half = K // 2
    first = jnp.dot(left_sparse[:, :half], right_sparse[:half], preferred_element_type=jnp.float32, precision=lax.Precision.HIGHEST)
    second = jnp.dot(left_sparse[:, half:], right_sparse[half:], preferred_element_type=jnp.float32, precision=lax.Precision.HIGHEST)
    return first + second
```

```python
import functools

import jax
import jax.numpy as jnp
from jax import lax
from jax.experimental import pallas as pl
from jax.experimental.pallas import tpu as pltpu
from jax.sharding import PartitionSpec as P


BLK = 64
KB = 4
JB = 16
LI, LQ = 2, 8
RCAP, LCAP = 12, 3
NZ, NC = 8, 8
SHARE = KB * BLK
COLS = JB * BLK
ROWS = 2 * LI * BLK
SLABS = RCAP // 2
LPACK = 96
F32, BF16 = jnp.float32, jnp.bfloat16
VMEM = pl.BlockSpec(memory_space=pltpu.VMEM)
SMEM = pl.BlockSpec(memory_space=pltpu.SMEM)
ANY = pl.BlockSpec(memory_space=pl.ANY)
PARAMS = pltpu.CompilerParams(vmem_limit_bytes=32 * 1024 * 1024)


def place():
    r = lax.axis_index("row")
    return lax.axis_index("layer"), r // 2, r % 2, lax.axis_index("col")


def low_half(shape):
    return lax.broadcasted_iota(jnp.int32, shape, 1) < BLK


def cost(flops, moved):
    return pl.CostEstimate(flops=flops, bytes_accessed=moved, transcendentals=0)


def block_at(ref, e, per_row, odd):
    k, j = e // per_row, e % per_row
    v = ref[
        pl.ds(pl.multiple_of(k * BLK, BLK), BLK),
        pl.ds(pl.multiple_of((j // 2) * 128, 128), 128),
    ]
    return jnp.where(j % 2 == odd, v, pltpu.roll(v, BLK, 1))


def pack_right(right, occupied, out, flags, index, sem):
    l, z, y, c = place()
    top = pl.multiple_of(l * 64 + z * 8, 8)
    copy = pltpu.make_async_copy(occupied.at[pl.ds(top, 8)], flags, sem)
    copy.start()
    copy.wait()
    count = jnp.int32(0)
    for k in range(KB):
        for j in range(JB):
            index[count] = k * JB + j
            count += flags[y * KB + k, c * JB + j]
    low = low_half((BLK, 128))
    for p in range(SLABS):
        ea = jnp.where(2 * p < count, index[2 * p], 0)
        eb = jnp.where(2 * p + 1 < count, index[2 * p + 1], 0)
        out[p * BLK : (p + 1) * BLK, :] = jnp.where(
            low, block_at(right, ea, JB, 0), block_at(right, eb, JB, 1)
        )


def pack_left(left, occupied, out, flags, index, sem):
    l, z, y, c = place()
    top = pl.multiple_of((z // 2) * 8, 8)
    copy = pltpu.make_async_copy(occupied.at[pl.ds(top, 8)], flags, sem)
    copy.start()
    copy.wait()
    count = jnp.int32(0)
    for i in range(LI):
        for q in range(LQ):
            index[count] = i * LQ + q
            count += flags[(z % 2) * 4 + y * LI + i, l * 64 + c * LQ + q]
    e = [jnp.where(s < count, index[s], 0) for s in range(LCAP)]
    low = low_half((BLK, 128))
    out[:BLK, :] = jnp.where(low, block_at(left, e[0], LQ, 0), block_at(left, e[1], LQ, 1))
    a = block_at(left, e[2], LQ, 0)
    b = block_at(left, e[2], LQ, 1)
    out[BLK:, :] = jnp.where(low_half((BLK // 2, 128)), a[: BLK // 2], b[BLK // 2 :])


def scan(left_occupied, right_occupied, left_index, right_index, lflags, rflags, sems):
    l, z, y, c = place()
    copies = [
        pltpu.make_async_copy(left_occupied.at[pl.ds(pl.multiple_of((z // 2) * 8, 8), 8)], lflags, sems.at[0]),
        pltpu.make_async_copy(right_occupied.at[pl.ds(pl.multiple_of(l * 64, 64), 64)], rflags, sems.at[1]),
    ]
    for copy in copies:
        copy.start()
    for copy in copies:
        copy.wait()

    @pl.loop(0, NZ)
    def _(s):
        for t in range(16):
            right_index[s, t] = -1
        count = jnp.int32(0)
        for k in range(KB):
            for j in range(JB):
                f = rflags[s * 8 + y * KB + k, c * JB + j]
                right_index[s, count] = jnp.where(f != 0, k * JB + j, -1)
                count += f

    @pl.loop(0, 2 * NC)
    def _(s):
        for t in range(4):
            left_index[s, t] = -1
        count = jnp.int32(0)
        for i in range(LI):
            for q in range(LQ):
                f = lflags[(z % 2) * 4 + (s // NC) * LI + i, l * 64 + (s % NC) * LQ + q]
                left_index[s, count] = jnp.where(f != 0, i * LQ + q, -1)
                count += f


def unpack_left(index, a0, a1, a2, a3, hi, lo, dense):
    l, z, y, c = place()
    x = c // 2
    dense[...] = jnp.zeros_like(dense)
    low = low_half((BLK, 128))
    for d, ref in enumerate((a0, a1, a2, a3)):
        for part in range(4):
            yh = (c % 2) ^ (part // 2)
            yl = y ^ (part % 2)
            column = ((x + d) % 4) * 2 + yh
            row = yl * NC + column
            for s in range(LCAP):
                e = index[row, s]
                i, q = e // LQ, e % LQ

                @pl.when((e >= 0) & (q // KB == y))
                def _(ref=ref, part=part, s=s, i=i, q=q, yl=yl, column=column):
                    base = part * LPACK
                    if s < 2:
                        v = ref[base : base + BLK, :]
                    else:
                        w = ref[base + BLK : base + LPACK, :]
                        v = jnp.concatenate([w, pltpu.roll(w, BLK, 1)], axis=0)
                    kk = q % KB
                    v = jnp.where(kk % 2 == s % 2, v, pltpu.roll(v, BLK, 1))
                    rows = pl.ds(pl.multiple_of(yl * 128 + i * BLK, BLK), BLK)
                    lanes = pl.ds(pl.multiple_of(column * SHARE + (kk // 2) * 128, 128), 128)
                    dense[rows, lanes] = jnp.where(low == (kk % 2 == 0), v, dense[rows, lanes])

    for t in range(0, NZ * SHARE, 128):
        v = dense[:, t : t + 128]
        h = v.astype(BF16)
        hi[:, t : t + 128] = h
        lo[:, t : t + 128] = (v - h.astype(F32)).astype(BF16)


def multiply(offsets, first, index, hi, lo, *refs):
    n = len(offsets)
    shares, refs = refs[:n], refs[n:]
    if not first:
        total, refs = refs[0], refs[1:]
    out, dense = refs
    l, z, y, c = place()
    low = low_half((BLK, 128))
    for t, (offset, share) in enumerate(zip(offsets, shares)):
        source = (z + offset) % NZ
        dense[...] = jnp.zeros_like(dense)
        for s in range(RCAP):
            e = index[source, s]

            @pl.when(e >= 0)
            def _(s=s, e=e, share=share):
                k, j = e // JB, e % JB
                p = s // 2
                v = share[p * BLK : (p + 1) * BLK, :]
                v = jnp.where(j % 2 == s % 2, v, pltpu.roll(v, BLK, 1))
                rows = pl.ds(pl.multiple_of(k * BLK, BLK), BLK)
                lanes = pl.ds(pl.multiple_of((j // 2) * 128, 128), 128)
                dense[rows, lanes] = jnp.where(low == (j % 2 == 0), v, dense[rows, lanes])

        ks = pl.ds(pl.multiple_of(source * SHARE, SHARE), SHARE)
        lh, ll = hi[:, ks], lo[:, ks]
        for n0 in range(0, COLS, 256):
            v = dense[:, n0 : n0 + 256]
            rh = v.astype(BF16)
            rl = (v - rh.astype(F32)).astype(BF16)
            dot = functools.partial(jnp.dot, preferred_element_type=F32)
            prod = dot(lh, rh) + (dot(lh, rl) + dot(ll, rh))
            if t > 0:
                prod += out[:, n0 : n0 + 256]
            elif not first:
                prod += total[:, n0 : n0 + 256]
            out[:, n0 : n0 + 256] = prod


def call_multiply(offsets, index, hi, lo, shares, total=None):
    first = total is None
    n = len(offsets)
    return pl.pallas_call(
        functools.partial(multiply, offsets, first),
        out_shape=jax.ShapeDtypeStruct((ROWS, COLS), F32),
        in_specs=[SMEM] + [VMEM] * (2 + n + (0 if first else 1)),
        out_specs=VMEM,
        scratch_shapes=[pltpu.VMEM((SHARE, COLS), F32)],
        compiler_params=PARAMS,
        cost_estimate=cost(n * 6 * ROWS * SHARE * COLS, 4 * ROWS * COLS),
    )(index, hi, lo, *shares, *(() if first else (total,)))


def z_perm(d):
    return [(z * 2 + y, ((z + d) % NZ) * 2 + y) for z in range(NZ) for y in range(2)]


def x_perm(d):
    return [(((x + d) % 4) * 2 + y, x * 2 + y) for x in range(4) for y in range(2)]


def local(left_tensor, right_tensor, left_occupied, right_occupied):
    l, z, y, c = place()
    right0 = pl.pallas_call(
        pack_right,
        out_shape=jax.ShapeDtypeStruct((SLABS * BLK, 128), F32),
        in_specs=[VMEM, ANY],
        out_specs=VMEM,
        scratch_shapes=[
            pltpu.SMEM((8, 128), jnp.int32),
            pltpu.SMEM((16,), jnp.int32),
            pltpu.SemaphoreType.DMA,
        ],
        compiler_params=PARAMS,
        cost_estimate=cost(0, 1 << 20),
    )(right_tensor, right_occupied)
    left0 = pl.pallas_call(
        pack_left,
        out_shape=jax.ShapeDtypeStruct((LPACK, 128), F32),
        in_specs=[VMEM, ANY],
        out_specs=VMEM,
        scratch_shapes=[
            pltpu.SMEM((8, 128), jnp.int32),
            pltpu.SMEM((16,), jnp.int32),
            pltpu.SemaphoreType.DMA,
        ],
        compiler_params=PARAMS,
        cost_estimate=cost(0, 1 << 18),
    )(left_tensor, left_occupied)
    left_index, right_index = pl.pallas_call(
        scan,
        out_shape=(
            jax.ShapeDtypeStruct((2 * NC, 8), jnp.int32),
            jax.ShapeDtypeStruct((NZ, 16), jnp.int32),
        ),
        in_specs=[ANY, ANY],
        out_specs=(SMEM, SMEM),
        scratch_shapes=[
            pltpu.SMEM((8, 128), jnp.int32),
            pltpu.SMEM((64, 128), jnp.int32),
            pltpu.SemaphoreType.DMA((2,)),
        ],
        compiler_params=PARAMS,
        cost_estimate=cost(0, 1 << 18),
    )(left_occupied, right_occupied)

    pair = [(r, r ^ 1) for r in range(16)]
    z_send = lambda v, d: lax.ppermute(v, "row", z_perm(d))
    up1, down1 = z_send(right0, 1), z_send(right0, -1)
    left1 = jnp.concatenate([left0, lax.ppermute(left0, "row", pair)])
    up2, down2 = z_send(up1, 1), z_send(down1, -1)
    left2 = jnp.concatenate([left1, lax.ppermute(left1, "col", [(r, r ^ 1) for r in range(8)])])
    up3, down3 = z_send(up2, 1), z_send(down2, -1)
    lefts = [left2] + [lax.ppermute(left2, "col", x_perm(d)) for d in (1, 2, 3)]
    half = SLABS * BLK // 2
    far = jnp.concatenate([z_send(up3[:half], 1), z_send(down3[half:], -1)])

    hi, lo = pl.pallas_call(
        unpack_left,
        out_shape=(jax.ShapeDtypeStruct((ROWS, NZ * SHARE), BF16),) * 2,
        in_specs=[SMEM] + [VMEM] * 4,
        out_specs=(VMEM, VMEM),
        scratch_shapes=[pltpu.VMEM((ROWS, NZ * SHARE), F32)],
        compiler_params=PARAMS,
        cost_estimate=cost(0, 1 << 22),
    )(left_index, *lefts)

    total = call_multiply((0, -1, 1), right_index, hi, lo, (right0, up1, down1))
    total = call_multiply((-2, 2), right_index, hi, lo, (up2, down2), total)
    total = call_multiply((-3, 3), right_index, hi, lo, (up3, down3), total)
    total = call_multiply((4,), right_index, hi, lo, (far,), total)

    width = COLS // 2
    swap = [(0, 1), (1, 0)]
    keep = lax.dynamic_slice(total, (0, l * width), (ROWS, width))
    give = lax.dynamic_slice(total, (0, (1 - l) * width), (ROWS, width))
    both = keep + lax.ppermute(give, "layer", swap)
    mine = lax.dynamic_slice(both, (y * 128, 0), (128, width))
    other = lax.dynamic_slice(both, ((1 - y) * 128, 0), (128, width))
    done = mine + lax.ppermute(other, "row", pair)
    rest = lax.ppermute(done, "layer", swap)
    return jnp.where(
        l == 0, jnp.concatenate([done, rest], axis=1), jnp.concatenate([rest, done], axis=1)
    )


def solution(mesh):
    placed = (P("row", ("layer", "col")), P(("layer", "row"), "col"), P(), P())
    return jax.shard_map(
        local, mesh=mesh, in_specs=placed, out_specs=P("row", "col"), check_vma=False
    )
```

```python
import functools

import jax
import jax.numpy as jnp
from jax import lax
from jax.experimental import pallas as pl
from jax.experimental.pallas import tpu as pltpu
from jax.sharding import PartitionSpec as P


BLK = 64
KB = 4
JB = 16
LI, LQ = 2, 8
RCAP, LCAP = 12, 3
NZ, NC = 8, 8
SHARE = KB * BLK
COLS = JB * BLK
ROWS = 2 * LI * BLK
SLABS = RCAP // 2
LPACK = 96
F32, BF16 = jnp.float32, jnp.bfloat16
VMEM = pl.BlockSpec(memory_space=pltpu.VMEM)
SMEM = pl.BlockSpec(memory_space=pltpu.SMEM)
ANY = pl.BlockSpec(memory_space=pl.ANY)
PARAMS = pltpu.CompilerParams(vmem_limit_bytes=32 * 1024 * 1024)


def place():
    r = lax.axis_index("row")
    return lax.axis_index("layer"), r // 2, r % 2, lax.axis_index("col")


def low_half(shape):
    return lax.broadcasted_iota(jnp.int32, shape, 1) < BLK


def cost(flops, moved):
    return pl.CostEstimate(flops=flops, bytes_accessed=moved, transcendentals=0)


def block_at(ref, e, per_row, odd):
    k, j = e // per_row, e % per_row
    v = ref[
        pl.ds(pl.multiple_of(k * BLK, BLK), BLK),
        pl.ds(pl.multiple_of((j // 2) * 128, 128), 128),
    ]
    return jnp.where(j % 2 == odd, v, pltpu.roll(v, BLK, 1))


def pack_right(right, occupied, out, flags, index, sem):
    l, z, y, c = place()
    top = pl.multiple_of(l * 64 + z * 8, 8)
    copy = pltpu.make_async_copy(occupied.at[pl.ds(top, 8)], flags, sem)
    copy.start()
    copy.wait()
    count = jnp.int32(0)
    for k in range(KB):
        for j in range(JB):
            index[count] = k * JB + j
            count += flags[y * KB + k, c * JB + j]
    low = low_half((BLK, 128))
    for p in range(SLABS):
        ea = jnp.where(2 * p < count, index[2 * p], 0)
        eb = jnp.where(2 * p + 1 < count, index[2 * p + 1], 0)
        out[p * BLK : (p + 1) * BLK, :] = jnp.where(
            low, block_at(right, ea, JB, 0), block_at(right, eb, JB, 1)
        )


def pack_left(left, occupied, out, flags, index, sem):
    l, z, y, c = place()
    top = pl.multiple_of((z // 2) * 8, 8)
    copy = pltpu.make_async_copy(occupied.at[pl.ds(top, 8)], flags, sem)
    copy.start()
    copy.wait()
    count = jnp.int32(0)
    for i in range(LI):
        for q in range(LQ):
            index[count] = i * LQ + q
            count += flags[(z % 2) * 4 + y * LI + i, l * 64 + c * LQ + q]
    e = [jnp.where(s < count, index[s], 0) for s in range(LCAP)]
    low = low_half((BLK, 128))
    out[:BLK, :] = jnp.where(low, block_at(left, e[0], LQ, 0), block_at(left, e[1], LQ, 1))
    a = block_at(left, e[2], LQ, 0)
    b = block_at(left, e[2], LQ, 1)
    out[BLK:, :] = jnp.where(low_half((BLK // 2, 128)), a[: BLK // 2], b[BLK // 2 :])


def tables(left_occupied, right_occupied, out, lflags, rflags, sems):
    l, z, y, c = place()
    copies = [
        pltpu.make_async_copy(left_occupied.at[pl.ds(pl.multiple_of((z // 2) * 8, 8), 8)], lflags, sems.at[0]),
        pltpu.make_async_copy(right_occupied.at[pl.ds(pl.multiple_of(l * 64, 64), 64)], rflags, sems.at[1]),
    ]
    for copy in copies:
        copy.start()
    for copy in copies:
        copy.wait()

    def grid(shape):
        return [lax.broadcasted_iota(jnp.int32, shape, d) for d in (0, 1)]

    def dot(a, b):
        return jnp.dot(a.astype(BF16), b.astype(BF16), preferred_element_type=F32)

    def slots(flags, per_row, rows):
        n = flags.shape[0]
        f = flags.astype(F32)
        a, b = grid((128, 128))
        same = a // per_row == b // per_row
        in_row = dot(f, (same & (a < b)).astype(F32))
        row_sum = dot(f, same.astype(F32))
        a, b = grid((n, n))
        before = dot(((a // rows == b // rows) & (b < a)).astype(F32), row_sum)
        a, b = grid((n, 128))
        rank = jnp.where(f > 0, in_row + before, -1.0)
        return rank, ((a % rows) * per_row + b % per_row + 1).astype(F32)

    a, b = grid((16, 64))
    fold = (a == b // KB).astype(F32)
    rank, number = slots(rflags[...], JB, KB)
    number = jnp.where(lax.broadcasted_iota(jnp.int32, (64, 128), 1) // JB == c, number, 0.0)
    a, b = grid((128, 128))
    total = jnp.full((16, 128), -1.0, F32)
    for t in range(RCAP):
        total += dot(dot(fold, jnp.where(rank == t, number, 0.0)), (b == t).astype(F32))
    out[:16, :] = total.astype(jnp.int32)

    g, h = grid((8, 8))
    fold = (g == h // LI).astype(F32)
    rank, number = slots(lflags[...], LQ, LI)
    total = jnp.full((8, 128), -1.0, F32)
    for t in range(LCAP):
        total += dot(dot(fold, jnp.where(rank == t, number, 0.0)), (b == (a // LQ) * 4 + t).astype(F32))
    out[16:, :] = total.astype(jnp.int32)


def unpack_left(index, a0, a1, a2, a3, out, dense):
    l, z, y, c = place()
    x = c // 2
    dense[...] = jnp.zeros_like(dense)
    low = low_half((BLK, 128))
    for d, ref in enumerate((a0, a1, a2, a3)):
        for part in range(4):
            yh = (c % 2) ^ (part // 2)
            yl = y ^ (part % 2)
            column = ((x + d) % 4) * 2 + yh
            for s in range(LCAP):
                e = index[16 + (z % 2) * 2 + yl, (l * NC + column) * 4 + s]
                i, q = e // LQ, e % LQ

                @pl.when((e >= 0) & (q // KB == y))
                def _(ref=ref, part=part, s=s, i=i, q=q, yl=yl, column=column):
                    base = part * LPACK
                    if s < 2:
                        v = ref[base : base + BLK, :]
                    else:
                        w = ref[base + BLK : base + LPACK, :]
                        v = jnp.concatenate([w, pltpu.roll(w, BLK, 1)], axis=0)
                    kk = q % KB
                    v = jnp.where(kk % 2 == s % 2, v, pltpu.roll(v, BLK, 1))
                    rows = pl.ds(pl.multiple_of(yl * 128 + i * BLK, BLK), BLK)
                    lanes = pl.ds(pl.multiple_of(column * SHARE + (kk // 2) * 128, 128), 128)
                    dense[rows, lanes] = jnp.where(low == (kk % 2 == 0), v, dense[rows, lanes])

    for t in range(0, NZ * SHARE, 128):
        v = dense[:, t : t + 128]
        h = v.astype(BF16)
        out[:ROWS, t : t + 128] = h
        out[ROWS:, t : t + 128] = (v - h.astype(F32)).astype(BF16)


def multiply(offsets, first, last, index, left, *refs):
    n = len(offsets)
    shares, refs = refs[:n], refs[n:]
    if not first:
        total, refs = refs[0], refs[1:]
    *outs, dense = refs
    l, z, y, c = place()
    low = low_half((BLK, 128))
    for t, (offset, share) in enumerate(zip(offsets, shares)):
        source = (z + offset) % NZ
        dense[t, :SHARE, :] = jnp.zeros((SHARE, COLS), F32)
        for s in range(RCAP):
            e = index[source * 2 + y, s]
            e = jnp.where(e < 0, KB * JB, e)
            k, j = e // JB, e % JB
            p = s // 2
            v = share[p * BLK : (p + 1) * BLK, :]
            v = jnp.where(j % 2 == s % 2, v, pltpu.roll(v, BLK, 1))
            rows = pl.ds(pl.multiple_of(k * BLK, BLK), BLK)
            lanes = pl.ds(pl.multiple_of((j // 2) * 128, 128), 128)
            dense[t, rows, lanes] = jnp.where(low == (j % 2 == 0), v, dense[t, rows, lanes])
    at = [pl.ds(pl.multiple_of(((z + o) % NZ) * SHARE, SHARE), SHARE) for o in offsets]
    dot = functools.partial(jnp.dot, preferred_element_type=F32)
    for n0 in range(0, COLS, 256):
        prod = None if first else total[:, n0 : n0 + 256]
        for t in range(n):
            v = dense[t, :SHARE, n0 : n0 + 256]
            rh = v.astype(BF16)
            rl = (v - rh.astype(F32)).astype(BF16)
            big = dot(left[:, at[t]], rh)
            one = (big[ROWS:] + dot(left[:ROWS, at[t]], rl)) + big[:ROWS]
            prod = one if prod is None else prod + one
        if last:
            keep, give = outs
            m = n0 % (COLS // 2)

            @pl.when((n0 >= COLS // 2) == (l == 1))
            def _(prod=prod, m=m):
                keep[:, m : m + 256] = prod

            @pl.when((n0 >= COLS // 2) != (l == 1))
            def _(prod=prod, m=m):
                give[:, m : m + 256] = prod
        else:
            outs[0][:, n0 : n0 + 256] = prod


def call_multiply(offsets, index, left, shares, total=None, last=False):
    first = total is None
    n = len(offsets)
    if last:
        shape, spec = (jax.ShapeDtypeStruct((ROWS, COLS // 2), F32),) * 2, (VMEM, VMEM)
    else:
        shape, spec = jax.ShapeDtypeStruct((ROWS, COLS), F32), VMEM
    return pl.pallas_call(
        functools.partial(multiply, offsets, first, last),
        out_shape=shape,
        in_specs=[SMEM] + [VMEM] * (1 + n + (0 if first else 1)),
        out_specs=spec,
        scratch_shapes=[pltpu.VMEM((n, SHARE + BLK, COLS), F32)],
        compiler_params=PARAMS,
        cost_estimate=cost(n * 6 * ROWS * SHARE * COLS, 4 * ROWS * COLS),
    )(index, left, *shares, *(() if first else (total,)))


def call_unpack(index, lefts):
    return pl.pallas_call(
        unpack_left,
        out_shape=jax.ShapeDtypeStruct((2 * ROWS, NZ * SHARE), BF16),
        in_specs=[SMEM] + [VMEM] * 4,
        out_specs=VMEM,
        scratch_shapes=[pltpu.VMEM((ROWS, NZ * SHARE), F32)],
        compiler_params=PARAMS,
        cost_estimate=cost(0, 1 << 22),
    )(index, *lefts)


def call_tables(left_occupied, right_occupied):
    return pl.pallas_call(
        tables,
        out_shape=jax.ShapeDtypeStruct((24, 128), jnp.int32),
        in_specs=[ANY, ANY],
        out_specs=VMEM,
        scratch_shapes=[
            pltpu.VMEM((8, 128), jnp.int32),
            pltpu.VMEM((64, 128), jnp.int32),
            pltpu.SemaphoreType.DMA((2,)),
        ],
        compiler_params=PARAMS,
        cost_estimate=cost(0, 1 << 18),
    )(left_occupied, right_occupied)


def call_pack(kernel, tensor, occupied, rows):
    return pl.pallas_call(
        kernel,
        out_shape=jax.ShapeDtypeStruct((rows, 128), F32),
        in_specs=[VMEM, ANY],
        out_specs=VMEM,
        scratch_shapes=[
            pltpu.SMEM((8, 128), jnp.int32),
            pltpu.SMEM((16,), jnp.int32),
            pltpu.SemaphoreType.DMA,
        ],
        compiler_params=PARAMS,
        cost_estimate=cost(0, 1 << 20),
    )(tensor, occupied)


def z_perm(d):
    return [(z * 2 + y, ((z + d) % NZ) * 2 + y) for z in range(NZ) for y in range(2)]


def x_perm(d):
    return [(((x + d) % 4) * 2 + y, x * 2 + y) for x in range(4) for y in range(2)]


def local(left_tensor, right_tensor, left_occupied, right_occupied):
    l, z, y, c = place()
    right0 = call_pack(pack_right, right_tensor, right_occupied, SLABS * BLK)
    left_tensor, right0 = lax.optimization_barrier((left_tensor, right0))
    left0 = call_pack(pack_left, left_tensor, left_occupied, LPACK)
    index = call_tables(left_occupied, right_occupied)

    pair = [(r, r ^ 1) for r in range(16)]
    z_send = lambda v, d: lax.ppermute(v, "row", z_perm(d))
    up1, down1 = z_send(right0, 1), z_send(right0, -1)
    left1 = jnp.concatenate([left0, lax.ppermute(left0, "row", pair)])
    up2, down2 = z_send(up1, 1), z_send(down1, -1)
    left2 = jnp.concatenate([left1, lax.ppermute(left1, "col", [(r, r ^ 1) for r in range(8)])])
    up3, down3 = z_send(up2, 1), z_send(down2, -1)
    lefts = [left2] + [lax.ppermute(left2, "col", x_perm(d)) for d in (1, 2, 3)]
    half = SLABS * BLK // 2
    far = jnp.concatenate([z_send(up3[:half], 1), z_send(down3[half:], -1)])

    left = call_unpack(index, lefts)
    total = call_multiply((0, -1, 1), index, left, (right0, up1, down1))
    total = call_multiply((-2, 2), index, left, (up2, down2), total)
    total = call_multiply((-3, 3), index, left, (up3, down3), total)
    keep, give = call_multiply((4,), index, left, (far,), total, last=True)

    width = COLS // 2
    swap = [(0, 1), (1, 0)]
    both = keep + lax.ppermute(give, "layer", swap)
    mine = lax.dynamic_slice(both, (y * 128, 0), (128, width))
    other = lax.dynamic_slice(both, ((1 - y) * 128, 0), (128, width))
    done = mine + lax.ppermute(other, "row", pair)
    rest = lax.ppermute(done, "layer", swap)
    return jnp.where(
        l == 0, jnp.concatenate([done, rest], axis=1), jnp.concatenate([rest, done], axis=1)
    )


def solution(mesh):
    placed = (P("row", ("layer", "col")), P(("layer", "row"), "col"), P(), P())
    return jax.shard_map(
        local, mesh=mesh, in_specs=placed, out_specs=P("row", "col"), check_vma=False
    )
```

```python
import functools

import jax
import jax.numpy as jnp
from jax import lax
from jax.experimental import pallas as pl
from jax.experimental.pallas import tpu as pltpu
from jax.sharding import PartitionSpec as P


BLK = 64
KB = 4
JB = 16
LI, LQ = 2, 8
RCAP, LCAP = 12, 3
NZ, NC = 8, 8
SHARE = KB * BLK
COLS = JB * BLK
ROWS = 2 * LI * BLK
SLABS = RCAP // 2
LPACK = 96
F32, BF16 = jnp.float32, jnp.bfloat16
VMEM = pl.BlockSpec(memory_space=pltpu.VMEM)
SMEM = pl.BlockSpec(memory_space=pltpu.SMEM)
HBM = pl.BlockSpec(memory_space=pltpu.HBM)
PARAMS = pltpu.CompilerParams(vmem_limit_bytes=32 * 1024 * 1024)
EMPTY = RCAP
HELD = (SLABS + 1) * BLK


def place():
    r = lax.axis_index("row")
    return lax.axis_index("layer"), r // 2, r % 2, lax.axis_index("col")


def low_half(shape):
    return lax.broadcasted_iota(jnp.int32, shape, 1) < BLK


def cost(flops, moved):
    return pl.CostEstimate(flops=flops, bytes_accessed=moved, transcendentals=0)


def block_at(ref, e, per_row, odd):
    k, j = e // per_row, e % per_row
    v = ref[
        pl.ds(pl.multiple_of(k * BLK, BLK), BLK),
        pl.ds(pl.multiple_of((j // 2) * 128, 128), 128),
    ]
    return jnp.where(j % 2 == odd, v, pltpu.roll(v, BLK, 1))


def pack(
    left_hbm, right_hbm, left_occupied, right_occupied, left_out, right_out,
    left, right, lflags, rflags, lindex, rindex, sems,
):
    l, z, y, c = place()
    ltop = pl.multiple_of((z // 2) * 8, 8)
    rtop = pl.multiple_of(l * 64 + z * 8, 8)
    copies = [
        pltpu.make_async_copy(right_occupied.at[pl.ds(rtop, 8)], rflags, sems.at[0]),
        pltpu.make_async_copy(left_occupied.at[pl.ds(ltop, 8)], lflags, sems.at[1]),
        pltpu.make_async_copy(right_hbm, right, sems.at[2]),
        pltpu.make_async_copy(left_hbm, left, sems.at[3]),
    ]
    for copy in copies:
        copy.start()
    copies[0].wait()
    rcount = jnp.int32(0)
    for k in range(KB):
        for j in range(JB):
            rindex[rcount] = k * JB + j
            rcount += rflags[y * KB + k, c * JB + j]
    copies[1].wait()
    lcount = jnp.int32(0)
    for i in range(LI):
        for q in range(LQ):
            lindex[lcount] = i * LQ + q
            lcount += lflags[(z % 2) * 4 + y * LI + i, l * 64 + c * LQ + q]
    low = low_half((BLK, 128))
    copies[2].wait()
    for p in range(SLABS):
        ea = jnp.where(2 * p < rcount, rindex[2 * p], 0)
        eb = jnp.where(2 * p + 1 < rcount, rindex[2 * p + 1], 0)
        right_out[p * BLK : (p + 1) * BLK, :] = jnp.where(
            low, block_at(right, ea, JB, 0), block_at(right, eb, JB, 1)
        )
    copies[3].wait()
    e = [jnp.where(s < lcount, lindex[s], 0) for s in range(LCAP)]
    left_out[:BLK, :] = jnp.where(low, block_at(left, e[0], LQ, 0), block_at(left, e[1], LQ, 1))
    a = block_at(left, e[2], LQ, 0)
    b = block_at(left, e[2], LQ, 1)
    left_out[BLK:, :] = jnp.where(low_half((BLK // 2, 128)), a[: BLK // 2], b[BLK // 2 :])


def tables(left_occupied, right_occupied, out, lflags, rflags, sems):
    l, z, y, c = place()
    copies = [
        pltpu.make_async_copy(left_occupied.at[pl.ds(pl.multiple_of((z // 2) * 8, 8), 8)], lflags, sems.at[0]),
        pltpu.make_async_copy(right_occupied.at[pl.ds(pl.multiple_of(l * 64, 64), 64)], rflags, sems.at[1]),
    ]
    for copy in copies:
        copy.start()
    for copy in copies:
        copy.wait()

    def grid(shape):
        return [lax.broadcasted_iota(jnp.int32, shape, d) for d in (0, 1)]

    def dot(a, b):
        return jnp.dot(a.astype(BF16), b.astype(BF16), preferred_element_type=F32)

    def ranks(flags, per_row, rows, none):
        n = flags.shape[0]
        f = flags.astype(F32)
        a, b = grid((128, 128))
        same = a // per_row == b // per_row
        in_row = dot(f, (same & (a < b)).astype(F32))
        row_sum = dot(f, same.astype(F32))
        a, b = grid((n, n))
        before = dot(((a // rows == b // rows) & (b < a)).astype(F32), row_sum)
        return jnp.where(f > 0, in_row + before, none)

    rank = ranks(rflags[...], JB, KB, float(EMPTY))
    a, b = grid((8, 64))
    g, h = grid((128, 128))
    total = jnp.zeros((8, 128), F32)
    for k in range(KB):
        row = dot((b == a * 8 + y * KB + k).astype(F32), rank)
        total += dot(row, ((h // JB == k) & (g == c * JB + h % JB)).astype(F32))
    out[:8, :] = total.astype(jnp.int32)

    rank = ranks(lflags[...], LQ, LI, -1.0)
    a, b = grid((8, 8))
    row = dot((b == (z % 2) * 4 + a).astype(F32), rank)
    row = dot(row, ((h < 32) & (g == l * 64 + (h // KB) * LQ + y * KB + h % KB)).astype(F32))
    out[8:, :] = row.astype(jnp.int32)


def split(v):
    h = v.astype(BF16)
    return h, (v - h.astype(F32)).astype(BF16)


def unpack_left(index, a0, a1, a2, a3, a4, out):
    l, z, y, c = place()
    x = c // 2
    low = low_half((BLK, 128))
    low2 = low_half((BLK // 2, 128))
    for d in range(4):
        for part in range(4):
            yh = (c % 2) ^ (part // 2)
            yl = y ^ (part % 2)
            column = ((x + d) % 4) * 2 + yh
            ref = (a0, a1, (a2, a3)[part // 2], a4)[d]
            base = (part % 2 if d == 2 else part) * LPACK
            v = ref[base : base + BLK, :]
            w = ref[base + BLK : base + LPACK, :]
            vr, wr = pltpu.roll(v, BLK, 1), pltpu.roll(w, BLK, 1)
            s0 = jnp.where(low, v, vr)
            s1 = jnp.where(low, vr, v)
            s2 = jnp.concatenate([jnp.where(low2, w, wr), jnp.where(low2, wr, w)], axis=0)
            for i in range(LI):
                for p in range(KB // 2):
                    at = column * KB + 2 * p
                    slot = jnp.where(low, index[8 + yl * LI + i, at], index[8 + yl * LI + i, at + 1])
                    t = jnp.where(slot == 0, s0, jnp.where(slot == 1, s1, jnp.where(slot == 2, s2, 0.0)))
                    lanes = pl.ds(pl.multiple_of(column * SHARE + p * 128, 128), 128)
                    top = pl.multiple_of(yl * 128 + i * BLK, BLK)
                    h, g = split(t)
                    out[pl.ds(top, BLK), lanes] = h
                    out[pl.ds(pl.multiple_of(ROWS + top, BLK), BLK), lanes] = g


def spread(index, source, share, two, hi, lo):
    low = low_half((BLK, 128))
    v = share[...]
    two[: SLABS * BLK, :] = v
    two[HELD : HELD + SLABS * BLK, :] = pltpu.roll(v, BLK, 1)
    two[SLABS * BLK : HELD, :] = jnp.zeros((BLK, 128), F32)
    two[HELD + SLABS * BLK :, :] = jnp.zeros((BLK, 128), F32)
    for k in range(KB):
        for p in range(JB // 2):
            s0 = index[source, k * JB + 2 * p]
            s1 = index[source, k * JB + 2 * p + 1]
            r0 = (s0 & 1) * HELD + lax.shift_right_logical(s0, 1) * BLK
            r1 = (1 - (s1 & 1)) * HELD + lax.shift_right_logical(s1, 1) * BLK
            v0 = two[pl.ds(pl.multiple_of(r0, BLK), BLK), :]
            v1 = two[pl.ds(pl.multiple_of(r1, BLK), BLK), :]
            h, g = split(jnp.where(low, v0, v1))
            hi[k * BLK : (k + 1) * BLK, p * 128 : (p + 1) * 128] = h
            lo[k * BLK : (k + 1) * BLK, p * 128 : (p + 1) * 128] = g


def unpack_right(offsets, index, *refs):
    n = len(offsets)
    shares, (hi, lo, two) = refs[:n], refs[n:]
    l, z, y, c = place()
    for t, offset in enumerate(offsets):
        spread(index, (z + offset) % NZ, shares[t], two.at[t], hi.at[t], lo.at[t])


def product(lhi, llo, rh, rl):
    dot = functools.partial(jnp.dot, preferred_element_type=F32)
    big = dot(jnp.concatenate([lhi, llo], axis=0), rh)
    n = lhi.shape[0]
    return (big[n:] + dot(lhi, rl)) + big[:n]


def multiply(groups, left, *refs):
    total = refs[-1]
    l, z, y, c = place()
    for n0 in range(0, COLS, 256):
        cols = slice(n0, n0 + 256)
        done = None
        for g, offsets in enumerate(groups):
            hi, lo = refs[2 * g : 2 * g + 2]
            for t, offset in enumerate(offsets):
                ks = pl.ds(pl.multiple_of(((z + offset) % NZ) * SHARE, SHARE), SHARE)
                one = product(left[:ROWS, ks], left[ROWS:, ks], hi[t, :, cols], lo[t, :, cols])
                done = one if done is None else done + one
        total[:, cols] = done


def finish(offset, mine, index, left, share, total, keep, give, two, hi, lo):
    l, z, y, c = place()
    source = (z + offset) % NZ
    spread(index, source, share, two, hi, lo)
    top = (y if mine else 1 - y) * 128
    rows = pl.ds(pl.multiple_of(top, 128), 128)
    ks = pl.ds(pl.multiple_of(source * SHARE, SHARE), SHARE)
    lhi, llo = left[rows, ks], left[pl.ds(pl.multiple_of(ROWS + top, 128), 128), ks]
    width = COLS // 2
    for out, first in ((give, (1 - l) * width), (keep, l * width)):
        for n0 in range(0, width, 256):
            cols = pl.ds(pl.multiple_of(first + n0, 256), 256)
            out[:, n0 : n0 + 256] = total[rows, cols] + product(lhi, llo, hi[:, cols], lo[:, cols])


def call_pack(*args):
    return pl.pallas_call(
        pack,
        out_shape=(
            jax.ShapeDtypeStruct((LPACK, 128), F32),
            jax.ShapeDtypeStruct((SLABS * BLK, 128), F32),
        ),
        in_specs=[HBM] * 4,
        out_specs=(VMEM, VMEM),
        scratch_shapes=[
            pltpu.VMEM((LI * BLK, LQ * BLK), F32),
            pltpu.VMEM((SHARE, COLS), F32),
            pltpu.SMEM((8, 128), jnp.int32),
            pltpu.SMEM((8, 128), jnp.int32),
            pltpu.SMEM((16,), jnp.int32),
            pltpu.SMEM((16,), jnp.int32),
            pltpu.SemaphoreType.DMA((4,)),
        ],
        compiler_params=PARAMS,
        cost_estimate=cost(0, 1 << 20),
    )(*args)


def call_tables(left_occupied, right_occupied):
    return pl.pallas_call(
        tables,
        out_shape=jax.ShapeDtypeStruct((16, 128), jnp.int32),
        in_specs=[HBM, HBM],
        out_specs=VMEM,
        scratch_shapes=[
            pltpu.VMEM((8, 128), jnp.int32),
            pltpu.VMEM((64, 128), jnp.int32),
            pltpu.SemaphoreType.DMA((2,)),
        ],
        compiler_params=PARAMS,
        cost_estimate=cost(0, 1 << 21),
    )(left_occupied, right_occupied)


def call_unpack_left(index, lefts):
    return pl.pallas_call(
        unpack_left,
        out_shape=jax.ShapeDtypeStruct((2 * ROWS, NZ * SHARE), BF16),
        in_specs=[SMEM] + [VMEM] * 5,
        out_specs=VMEM,
        compiler_params=PARAMS,
        cost_estimate=cost(0, 1 << 22),
    )(index, *lefts)


def call_unpack_right(offsets, index, shares):
    n = len(offsets)
    return pl.pallas_call(
        functools.partial(unpack_right, offsets),
        out_shape=(jax.ShapeDtypeStruct((n, SHARE, COLS), BF16),) * 2,
        in_specs=[SMEM] + [VMEM] * n,
        out_specs=(VMEM, VMEM),
        scratch_shapes=[pltpu.VMEM((n, 2 * HELD, 128), F32)],
        compiler_params=PARAMS,
        cost_estimate=cost(0, n << 20),
    )(index, *shares)


def call_multiply(groups, left, rights):
    n = sum(len(g) for g in groups)
    return pl.pallas_call(
        functools.partial(multiply, groups),
        out_shape=jax.ShapeDtypeStruct((ROWS, COLS), F32),
        in_specs=[VMEM] * (1 + len(rights)),
        out_specs=VMEM,
        compiler_params=PARAMS,
        cost_estimate=cost(n * 6 * ROWS * SHARE * COLS, 4 * ROWS * COLS),
    )(left, *rights)


def call_finish(offset, mine, index, left, share, total):
    return pl.pallas_call(
        functools.partial(finish, offset, mine),
        out_shape=(jax.ShapeDtypeStruct((128, COLS // 2), F32),) * 2,
        in_specs=[SMEM] + [VMEM] * 3,
        out_specs=(VMEM, VMEM),
        scratch_shapes=[
            pltpu.VMEM((2 * HELD, 128), F32),
            pltpu.VMEM((SHARE, COLS), BF16),
            pltpu.VMEM((SHARE, COLS), BF16),
        ],
        compiler_params=PARAMS,
        cost_estimate=cost(3 * ROWS * SHARE * COLS, 4 * ROWS * COLS),
    )(index, left, share, total)


def z_perm(d):
    return [(z * 2 + y, ((z + d) % NZ) * 2 + y) for z in range(NZ) for y in range(2)]


def x_perm(d):
    return [(((x + d) % 4) * 2 + y, x * 2 + y) for x in range(4) for y in range(2)]


def local(left_tensor, right_tensor, left_occupied, right_occupied):
    l = lax.axis_index("layer")
    left0, right0 = call_pack(left_tensor, right_tensor, left_occupied, right_occupied)
    index = call_tables(left_occupied, right_occupied)

    pair = [(r, r ^ 1) for r in range(16)]
    near = lambda dy, dh: [(r * 8 + c, (r ^ dy) * 8 + (c ^ dh)) for r in range(16) for c in range(8)]
    z_send = lambda v, d: lax.ppermute(v, "row", z_perm(d))
    up1, down1 = z_send(right0, 1), z_send(right0, -1)
    left2 = jnp.concatenate(
        [left0]
        + [lax.ppermute(left0, ("row", "col"), near(dy, dh)) for dy, dh in ((1, 0), (0, 1), (1, 1))]
    )
    (up1, down1, index) = lax.optimization_barrier((up1, down1, index))
    up2, down2 = z_send(up1, 1), z_send(down1, -1)
    rights1 = call_unpack_right((0, -1, 1), index, (right0, up1, down1))
    x_send = lambda v, d: lax.ppermute(v, "col", x_perm(d))
    cut = 2 * LPACK
    lefts = [left2, x_send(left2, 1), x_send(left2[:cut], 2), x_send(left2[cut:], -2), x_send(left2, -1)]
    up3, down3 = z_send(up2, 1), z_send(down2, -1)
    rights2 = call_unpack_right((-2, 2), index, (up2, down2))
    half = SLABS * BLK // 2
    far = jnp.concatenate([z_send(up3[:half], 1), z_send(down3[half:], -1)])
    rights3 = call_unpack_right((-3, 3), index, (up3, down3))

    left = call_unpack_left(index, lefts)
    total = call_multiply(((0, -1, 1), (-2, 2), (-3, 3)), left, rights1 + rights2 + rights3)
    keep, give = call_finish(4, False, index, left, far, total)

    swap = [(0, 1), (1, 0)]
    other = keep + lax.ppermute(give, "layer", swap)
    keep, give = call_finish(4, True, index, left, far, total)
    mine = keep + lax.ppermute(give, "layer", swap)
    done = mine + lax.ppermute(other, "row", pair)
    rest = lax.ppermute(done, "layer", swap)
    return jnp.where(
        l == 0, jnp.concatenate([done, rest], axis=1), jnp.concatenate([rest, done], axis=1)
    )


def solution(mesh):
    placed = (P("row", ("layer", "col")), P(("layer", "row"), "col"), P(), P())
    return jax.shard_map(
        local, mesh=mesh, in_specs=placed, out_specs=P("row", "col"), check_vma=False
    )
```

```python
import functools

import jax
import jax.numpy as jnp
from jax import lax
from jax.experimental import pallas as pl
from jax.experimental.pallas import tpu as pltpu
from jax.sharding import PartitionSpec as P


BLK = 64
KB = 4
JB = 16
LI, LQ = 2, 8
RCAP, LCAP = 12, 3
NZ, NC = 8, 8
SHARE = KB * BLK
COLS = JB * BLK
ROWS = 2 * LI * BLK
SLABS = RCAP // 2
LPACK = 96
F32, BF16 = jnp.float32, jnp.bfloat16
VMEM = pl.BlockSpec(memory_space=pltpu.VMEM)
SMEM = pl.BlockSpec(memory_space=pltpu.SMEM)
HBM = pl.BlockSpec(memory_space=pltpu.HBM)
ALONE = pltpu.CompilerParams(vmem_limit_bytes=60 * 1024 * 1024)
PARAMS = pltpu.CompilerParams(vmem_limit_bytes=32 * 1024 * 1024)
EMPTY = RCAP
HELD = (SLABS + 1) * BLK


def place():
    r = lax.axis_index("row")
    return lax.axis_index("layer"), r // 2, r % 2, lax.axis_index("col")


def low_half(shape):
    return lax.broadcasted_iota(jnp.int32, shape, 1) < BLK


def cost(flops, moved):
    return pl.CostEstimate(flops=flops, bytes_accessed=moved, transcendentals=0)


def block_at(ref, e, per_row, odd):
    k, j = e // per_row, e % per_row
    v = ref[
        pl.ds(pl.multiple_of(k * BLK, BLK), BLK),
        pl.ds(pl.multiple_of((j // 2) * 128, 128), 128),
    ]
    return jnp.where(j % 2 == odd, v, pltpu.roll(v, BLK, 1))


def ranks(flags, per_row, rows, none):
    n = flags.shape[0]
    f = flags.astype(F32)
    a, b = grid((128, 128))
    same = a // per_row == b // per_row
    in_row = pick(f, same & (a < b))
    row_sum = pick(f, same)
    a, b = grid((n, n))
    before = pick((a // rows == b // rows) & (b < a), row_sum)
    return jnp.where(f > 0, in_row + before, none)


def grid(shape):
    return [lax.broadcasted_iota(jnp.int32, shape, d) for d in (0, 1)]


def pick(a, b):
    return jnp.dot(
        a.astype(F32).astype(BF16), b.astype(F32).astype(BF16), preferred_element_type=F32
    )


def pack(
    left_hbm, right_hbm, left_occupied, right_occupied, left_out, right_out, slots,
    left, right, lflags, rflags, lindex, rindex, lall, rall, sems,
):
    l, z, y, c = place()
    ltop = pl.multiple_of((z // 2) * 8, 8)
    rtop = pl.multiple_of(l * 64 + z * 8, 8)
    ptop = pl.multiple_of(l * 64, 64)
    copies = [
        pltpu.make_async_copy(right_occupied.at[pl.ds(rtop, 8)], rflags, sems.at[0]),
        pltpu.make_async_copy(left_occupied.at[pl.ds(ltop, 8)], lflags, sems.at[1]),
        pltpu.make_async_copy(right_hbm, right, sems.at[2]),
        pltpu.make_async_copy(left_hbm, left, sems.at[3]),
        pltpu.make_async_copy(right_occupied.at[pl.ds(ptop, 64)], rall, sems.at[4]),
        pltpu.make_async_copy(left_occupied.at[pl.ds(ltop, 8)], lall, sems.at[5]),
    ]
    for copy in copies:
        copy.start()
    copies[0].wait()
    rcount = jnp.int32(0)
    for k in range(KB):
        for j in range(JB):
            rindex[rcount] = k * JB + j
            rcount += rflags[y * KB + k, c * JB + j]
    copies[1].wait()
    lcount = jnp.int32(0)
    for i in range(LI):
        for q in range(LQ):
            lindex[lcount] = i * LQ + q
            lcount += lflags[(z % 2) * 4 + y * LI + i, l * 64 + c * LQ + q]
    copies[4].wait()
    copies[5].wait()
    rank = ranks(rall[...], JB, KB, float(EMPTY))
    a, b = grid((8, 64))
    g, h = grid((128, 128))
    total = jnp.zeros((8, 128), F32)
    for k in range(KB):
        row = pick(b == a * 8 + y * KB + k, rank)
        total += pick(row, (h // JB == k) & (g == c * JB + h % JB))
    slots[:8, :] = total.astype(jnp.int32)
    rank = ranks(lall[...], LQ, LI, -1.0)
    a, b = grid((8, 8))
    row = pick(b == (z % 2) * 4 + a, rank)
    row = pick(row, (h < 32) & (g == l * 64 + (h // KB) * LQ + y * KB + h % KB))
    slots[8:, :] = row.astype(jnp.int32)
    low = low_half((BLK, 128))
    copies[2].wait()
    for p in range(SLABS):
        ea = jnp.where(2 * p < rcount, rindex[2 * p], 0)
        eb = jnp.where(2 * p + 1 < rcount, rindex[2 * p + 1], 0)
        right_out[p * BLK : (p + 1) * BLK, :] = jnp.where(
            low, block_at(right, ea, JB, 0), block_at(right, eb, JB, 1)
        )
    copies[3].wait()
    e = [jnp.where(s < lcount, lindex[s], 0) for s in range(LCAP)]
    left_out[:BLK, :] = jnp.where(low, block_at(left, e[0], LQ, 0), block_at(left, e[1], LQ, 1))
    a = block_at(left, e[2], LQ, 0)
    b = block_at(left, e[2], LQ, 1)
    left_out[BLK:, :] = jnp.where(low_half((BLK // 2, 128)), a[: BLK // 2], b[BLK // 2 :])


def join(*refs):
    *parts, out = refs
    for t, part in enumerate(parts):
        out[t * LPACK : (t + 1) * LPACK, :] = part[...]


def split(v):
    h = v.astype(BF16)
    return h, (v - h.astype(F32)).astype(BF16)


def unpack_left(index, a0, a1, a2, a3, out):
    l, z, y, c = place()
    x = c // 2
    low = low_half((BLK, 128))
    low2 = low_half((BLK // 2, 128))
    for d, ref in enumerate((a0, a1, a2, a3)):
        for part in range(4):
            yh = (c % 2) ^ (part // 2)
            yl = y ^ (part % 2)
            column = ((x + d) % 4) * 2 + yh
            base = part * LPACK
            v = ref[base : base + BLK, :]
            w = ref[base + BLK : base + LPACK, :]
            vr, wr = pltpu.roll(v, BLK, 1), pltpu.roll(w, BLK, 1)
            s0 = jnp.where(low, v, vr)
            s1 = jnp.where(low, vr, v)
            s2 = jnp.concatenate([jnp.where(low2, w, wr), jnp.where(low2, wr, w)], axis=0)
            for i in range(LI):
                for p in range(KB // 2):
                    at = column * KB + 2 * p
                    slot = jnp.where(low, index[8 + yl * LI + i, at], index[8 + yl * LI + i, at + 1])
                    t = jnp.where(slot == 0, s0, jnp.where(slot == 1, s1, jnp.where(slot == 2, s2, 0.0)))
                    lanes = pl.ds(pl.multiple_of(column * SHARE + p * 128, 128), 128)
                    top = pl.multiple_of(yl * 128 + i * BLK, BLK)
                    h, g = split(t)
                    out[pl.ds(top, BLK), lanes] = h
                    out[pl.ds(pl.multiple_of(ROWS + top, BLK), BLK), lanes] = g


def spread(index, source, pieces, two, hi, lo):
    low = low_half((BLK, 128))
    top = 0
    for piece in pieces:
        v = piece[...]
        n = v.shape[0]
        two[top : top + n, :] = v
        two[HELD + top : HELD + top + n, :] = pltpu.roll(v, BLK, 1)
        top += n
    two[SLABS * BLK : HELD, :] = jnp.zeros((BLK, 128), F32)
    two[HELD + SLABS * BLK :, :] = jnp.zeros((BLK, 128), F32)
    for k in range(KB):
        for p in range(JB // 2):
            s0 = index[source, k * JB + 2 * p]
            s1 = index[source, k * JB + 2 * p + 1]
            r0 = (s0 & 1) * HELD + lax.shift_right_logical(s0, 1) * BLK
            r1 = (1 - (s1 & 1)) * HELD + lax.shift_right_logical(s1, 1) * BLK
            v0 = two[pl.ds(pl.multiple_of(r0, BLK), BLK), :]
            v1 = two[pl.ds(pl.multiple_of(r1, BLK), BLK), :]
            h, g = split(jnp.where(low, v0, v1))
            hi[k * BLK : (k + 1) * BLK, p * 128 : (p + 1) * 128] = h
            lo[k * BLK : (k + 1) * BLK, p * 128 : (p + 1) * 128] = g


def unpack_right(offsets, index, *refs):
    n = len(offsets)
    shares, (hi, lo, two) = refs[:n], refs[n:]
    l, z, y, c = place()
    for t, offset in enumerate(offsets):
        spread(index, (z + offset) % NZ, shares[t : t + 1], two.at[t], hi.at[t], lo.at[t])


def product(lhi, llo, rh, rl):
    dot = functools.partial(jnp.dot, preferred_element_type=F32)
    big = dot(jnp.concatenate([lhi, llo], axis=0), rh)
    n = lhi.shape[0]
    return (big[n:] + dot(lhi, rl)) + big[:n]


def multiply(ready, fresh, index, left, *refs):
    (hi, lo), shares, (total, two, fhi, flo) = refs[:2], refs[2:-4], refs[-4:]
    l, z, y, c = place()
    parts = [(offset, hi.at[t], lo.at[t]) for t, offset in enumerate(ready)]
    for t, offset in enumerate(fresh):
        spread(index, (z + offset) % NZ, shares[t : t + 1], two.at[t], fhi.at[t], flo.at[t])
        parts.append((offset, fhi.at[t], flo.at[t]))
    for n0 in range(0, COLS, 256):
        cols = slice(n0, n0 + 256)
        done = None
        for offset, h, g in parts:
            ks = pl.ds(pl.multiple_of(((z + offset) % NZ) * SHARE, SHARE), SHARE)
            one = product(left[:ROWS, ks], left[ROWS:, ks], h[:, cols], g[:, cols])
            done = one if done is None else done + one
        total[:, cols] = done


def finish(offset, mine, index, left, share0, share1, total, *refs):
    *outs, two, hi, lo = refs
    l, z, y, c = place()
    source = (z + offset) % NZ
    spread(index, source, (share0, share1), two, hi, lo)
    top = (y if mine else 1 - y) * 128
    rows = pl.ds(pl.multiple_of(top, 128), 128)
    ks = pl.ds(pl.multiple_of(source * SHARE, SHARE), SHARE)
    lhi, llo = left[rows, ks], left[pl.ds(pl.multiple_of(ROWS + top, 128), 128), ks]
    if mine:
        for n0 in range(0, COLS, 256):
            cols = slice(n0, n0 + 256)
            outs[0][:, cols] = total[rows, cols] + product(lhi, llo, hi[:, cols], lo[:, cols])
        return
    width = COLS // 2
    for out, first in zip(outs, (l * width, (1 - l) * width)):
        for n0 in range(0, width, 256):
            cols = pl.ds(pl.multiple_of(first + n0, 256), 256)
            out[:, n0 : n0 + 256] = total[rows, cols] + product(lhi, llo, hi[:, cols], lo[:, cols])


def call_pack(*args):
    return pl.pallas_call(
        pack,
        out_shape=(
            jax.ShapeDtypeStruct((LPACK, 128), F32),
            jax.ShapeDtypeStruct((SLABS * BLK, 128), F32),
            jax.ShapeDtypeStruct((16, 128), jnp.int32),
        ),
        in_specs=[HBM] * 4,
        out_specs=(VMEM, VMEM, VMEM),
        scratch_shapes=[
            pltpu.VMEM((LI * BLK, LQ * BLK), F32),
            pltpu.VMEM((SHARE, COLS), F32),
            pltpu.SMEM((8, 128), jnp.int32),
            pltpu.SMEM((8, 128), jnp.int32),
            pltpu.SMEM((16,), jnp.int32),
            pltpu.SMEM((16,), jnp.int32),
            pltpu.VMEM((8, 128), jnp.int32),
            pltpu.VMEM((64, 128), jnp.int32),
            pltpu.SemaphoreType.DMA((6,)),
        ],
        compiler_params=ALONE,
        cost_estimate=cost(0, 1 << 20),
    )(*args)


def call_join(parts):
    return pl.pallas_call(
        join,
        out_shape=jax.ShapeDtypeStruct((len(parts) * LPACK, 128), F32),
        in_specs=[VMEM] * len(parts),
        out_specs=VMEM,
        compiler_params=PARAMS,
        cost_estimate=cost(0, 1 << 18),
    )(*parts)


def call_unpack_left(index, lefts):
    return pl.pallas_call(
        unpack_left,
        out_shape=jax.ShapeDtypeStruct((2 * ROWS, NZ * SHARE), BF16),
        in_specs=[SMEM] + [VMEM] * 4,
        out_specs=VMEM,
        compiler_params=PARAMS,
        cost_estimate=cost(0, 1 << 16),
    )(index, *lefts)


def call_unpack_right(offsets, index, shares):
    n = len(offsets)
    return pl.pallas_call(
        functools.partial(unpack_right, offsets),
        out_shape=(jax.ShapeDtypeStruct((n, SHARE, COLS), BF16),) * 2,
        in_specs=[SMEM] + [VMEM] * n,
        out_specs=(VMEM, VMEM),
        scratch_shapes=[pltpu.VMEM((n, 2 * HELD, 128), F32)],
        compiler_params=PARAMS,
        cost_estimate=cost(0, n << 20),
    )(index, *shares)


def call_multiply(ready, fresh, index, left, rights, shares):
    n = len(fresh)
    return pl.pallas_call(
        functools.partial(multiply, ready, fresh),
        out_shape=jax.ShapeDtypeStruct((ROWS, COLS), F32),
        in_specs=[SMEM] + [VMEM] * (3 + n),
        out_specs=VMEM,
        scratch_shapes=[
            pltpu.VMEM((n, 2 * HELD, 128), F32),
            pltpu.VMEM((n, SHARE, COLS), BF16),
            pltpu.VMEM((n, SHARE, COLS), BF16),
        ],
        compiler_params=PARAMS,
        cost_estimate=cost((len(ready) + n) * 6 * ROWS * SHARE * COLS, 4 * ROWS * COLS),
    )(index, left, *rights, *shares)


def call_finish(offset, mine, index, left, shares, total):
    shape = jax.ShapeDtypeStruct((128, COLS if mine else COLS // 2), F32)
    return pl.pallas_call(
        functools.partial(finish, offset, mine),
        out_shape=shape if mine else (shape, shape),
        in_specs=[SMEM] + [VMEM] * 4,
        out_specs=VMEM if mine else (VMEM, VMEM),
        scratch_shapes=[
            pltpu.VMEM((2 * HELD, 128), F32),
            pltpu.VMEM((SHARE, COLS), BF16),
            pltpu.VMEM((SHARE, COLS), BF16),
        ],
        compiler_params=PARAMS,
        cost_estimate=cost(3 * ROWS * SHARE * COLS, 4 * ROWS * COLS),
    )(index, left, *shares, total)


def z_perm(d):
    return [(z * 2 + y, ((z + d) % NZ) * 2 + y) for z in range(NZ) for y in range(2)]


def x_perm(d):
    return [(((x + d) % 4) * 2 + y, x * 2 + y) for x in range(4) for y in range(2)]


def local(left_tensor, right_tensor, left_occupied, right_occupied):
    l = lax.axis_index("layer")
    left0, right0, index = call_pack(left_tensor, right_tensor, left_occupied, right_occupied)

    pair = [(r, r ^ 1) for r in range(16)]
    near = lambda dy, dh: [(r * 8 + c, (r ^ dy) * 8 + (c ^ dh)) for r in range(16) for c in range(8)]
    z_send = lambda v, d: lax.ppermute(v, "row", z_perm(d))
    up1, down1 = z_send(right0, 1), z_send(right0, -1)
    left2 = call_join(
        [left0]
        + [lax.ppermute(left0, ("row", "col"), near(dy, dh)) for dy, dh in ((1, 0), (0, 1), (1, 1))]
    )
    up1, down1, left2 = lax.optimization_barrier((up1, down1, left2))
    up2, down2 = z_send(up1, 1), z_send(down1, -1)
    x_send = lambda v, d: lax.ppermute(v, "col", x_perm(d))
    lefts = [left2] + [x_send(left2, d) for d in (1, 2, 3)]
    up3, down3 = z_send(up2, 1), z_send(down2, -1)
    ready = (0, -1, 1, -2, 2)
    rights = call_unpack_right(ready, index, (right0, up1, down1, up2, down2))
    half = SLABS * BLK // 2
    far = z_send(up3[:half], 1), z_send(down3[half:], -1)

    left = call_unpack_left(index, lefts)
    total = call_multiply(ready, (-3, 3), index, left, rights, (up3, down3))
    swap = [(0, 1), (1, 0)]
    keep, give = call_finish(4, False, index, left, far, total)
    send = keep + lax.ppermute(give, "layer", swap)
    other = lax.ppermute(send, "row", pair)
    total, send = lax.optimization_barrier((total, send))
    mine = call_finish(4, True, index, left, far, total)
    mine += lax.ppermute(mine, "layer", swap)
    rest = lax.ppermute(other, "layer", swap)
    return mine + jnp.where(
        l == 0, jnp.concatenate([other, rest], axis=1), jnp.concatenate([rest, other], axis=1)
    )


def solution(mesh):
    placed = (P("row", ("layer", "col")), P(("layer", "row"), "col"), P(), P())
    return jax.shard_map(
        local, mesh=mesh, in_specs=placed, out_specs=P("row", "col"), check_vma=False
    )
```

```python
import functools

import jax
import jax.numpy as jnp
from jax import lax
from jax.experimental import pallas as pl
from jax.experimental.pallas import tpu as pltpu
from jax.sharding import PartitionSpec as P


BLK = 64
KB = 4
JB = 16
LI, LQ = 2, 8
RCAP, LCAP = 12, 3
NZ, NC = 8, 8
SHARE = KB * BLK
COLS = JB * BLK
ROWS = 2 * LI * BLK
SLABS = RCAP // 2
LPACK = 96
F32, BF16 = jnp.float32, jnp.bfloat16
VMEM = pl.BlockSpec(memory_space=pltpu.VMEM)
SMEM = pl.BlockSpec(memory_space=pltpu.SMEM)
HBM = pl.BlockSpec(memory_space=pltpu.HBM)
ALONE = pltpu.CompilerParams(vmem_limit_bytes=60 * 1024 * 1024)
PARAMS = pltpu.CompilerParams(vmem_limit_bytes=32 * 1024 * 1024)
EMPTY = RCAP
HELD = (SLABS + 1) * BLK


def place():
    r = lax.axis_index("row")
    return lax.axis_index("layer"), r // 2, r % 2, lax.axis_index("col")


def low_half(shape):
    return lax.broadcasted_iota(jnp.int32, shape, 1) < BLK


def cost(flops, moved):
    return pl.CostEstimate(flops=flops, bytes_accessed=moved, transcendentals=0)


def block_at(ref, e, per_row, odd):
    k, j = e // per_row, e % per_row
    v = ref[
        pl.ds(pl.multiple_of(k * BLK, BLK), BLK),
        pl.ds(pl.multiple_of((j // 2) * 128, 128), 128),
    ]
    return jnp.where(j % 2 == odd, v, pltpu.roll(v, BLK, 1))


def ranks(flags, per_row, rows, none):
    n = flags.shape[0]
    f = flags.astype(F32)
    a, b = grid((128, 128))
    same = a // per_row == b // per_row
    in_row = pick(f, same & (a < b))
    row_sum = pick(f, same)
    a, b = grid((n, n))
    before = pick((a // rows == b // rows) & (b < a), row_sum)
    return jnp.where(f > 0, in_row + before, none)


def grid(shape):
    return [lax.broadcasted_iota(jnp.int32, shape, d) for d in (0, 1)]


def pick(a, b):
    return jnp.dot(
        a.astype(F32).astype(BF16), b.astype(F32).astype(BF16), preferred_element_type=F32
    )


def pack(
    left_hbm, right_hbm, left_occupied, right_occupied, left_out, right_out, slots,
    left, right, lflags, rflags, lindex, rindex, lall, rall, sems,
):
    l, z, y, c = place()
    ltop = pl.multiple_of((z // 2) * 8, 8)
    rtop = pl.multiple_of(l * 64 + z * 8, 8)
    ptop = pl.multiple_of(l * 64, 64)
    copies = [
        pltpu.make_async_copy(right_occupied.at[pl.ds(rtop, 8)], rflags, sems.at[0]),
        pltpu.make_async_copy(left_occupied.at[pl.ds(ltop, 8)], lflags, sems.at[1]),
        pltpu.make_async_copy(right_hbm, right, sems.at[2]),
        pltpu.make_async_copy(left_hbm, left, sems.at[3]),
        pltpu.make_async_copy(right_occupied.at[pl.ds(ptop, 64)], rall, sems.at[4]),
        pltpu.make_async_copy(left_occupied.at[pl.ds(ltop, 8)], lall, sems.at[5]),
    ]
    for copy in copies:
        copy.start()
    copies[0].wait()
    rcount = jnp.int32(0)
    for k in range(KB):
        for j in range(JB):
            rindex[rcount] = k * JB + j
            rcount += rflags[y * KB + k, c * JB + j]
    copies[1].wait()
    lcount = jnp.int32(0)
    for i in range(LI):
        for q in range(LQ):
            lindex[lcount] = i * LQ + q
            lcount += lflags[(z % 2) * 4 + y * LI + i, l * 64 + c * LQ + q]
    copies[4].wait()
    copies[5].wait()
    rank = ranks(rall[...], JB, KB, float(EMPTY))
    a, b = grid((8, 64))
    g, h = grid((128, 128))
    total = jnp.zeros((8, 128), F32)
    for k in range(KB):
        row = pick(b == a * 8 + y * KB + k, rank)
        total += pick(row, (h // JB == k) & (g == c * JB + h % JB))
    slots[:8, :] = total.astype(jnp.int32)
    rank = ranks(lall[...], LQ, LI, -1.0)
    a, b = grid((8, 8))
    row = pick(b == (z % 2) * 4 + a, rank)
    row = pick(row, (h < 32) & (g == l * 64 + (h // KB) * LQ + y * KB + h % KB))
    slots[8:, :] = row.astype(jnp.int32)
    low = low_half((BLK, 128))
    copies[2].wait()
    for p in range(SLABS):
        ea = jnp.where(2 * p < rcount, rindex[2 * p], 0)
        eb = jnp.where(2 * p + 1 < rcount, rindex[2 * p + 1], 0)
        right_out[p * BLK : (p + 1) * BLK, :] = jnp.where(
            low, block_at(right, ea, JB, 0), block_at(right, eb, JB, 1)
        )
    copies[3].wait()
    e = [jnp.where(s < lcount, lindex[s], 0) for s in range(LCAP)]
    left_out[:BLK, :] = jnp.where(low, block_at(left, e[0], LQ, 0), block_at(left, e[1], LQ, 1))
    a = block_at(left, e[2], LQ, 0)
    b = block_at(left, e[2], LQ, 1)
    left_out[BLK:, :] = jnp.where(low_half((BLK // 2, 128)), a[: BLK // 2], b[BLK // 2 :])


def join(*refs):
    *parts, out = refs
    for t, part in enumerate(parts):
        out[t * LPACK : (t + 1) * LPACK, :] = part[...]


def split(v):
    h = v.astype(BF16)
    return h, (v - h.astype(F32)).astype(BF16)


def unpack_left(index, a0, a1, a2, a3, out):
    l, z, y, c = place()
    x = c // 2
    low = low_half((BLK, 128))
    low2 = low_half((BLK // 2, 128))
    for d, ref in enumerate((a0, a1, a2, a3)):
        for part in range(4):
            yh = (c % 2) ^ (part // 2)
            yl = y ^ (part % 2)
            column = ((x + d) % 4) * 2 + yh
            base = part * LPACK
            v = ref[base : base + BLK, :]
            w = ref[base + BLK : base + LPACK, :]
            vr, wr = pltpu.roll(v, BLK, 1), pltpu.roll(w, BLK, 1)
            s0 = jnp.where(low, v, vr)
            s1 = jnp.where(low, vr, v)
            s2 = jnp.concatenate([jnp.where(low2, w, wr), jnp.where(low2, wr, w)], axis=0)
            for i in range(LI):
                for p in range(KB // 2):
                    at = column * KB + 2 * p
                    slot = jnp.where(low, index[8 + yl * LI + i, at], index[8 + yl * LI + i, at + 1])
                    t = jnp.where(slot == 0, s0, jnp.where(slot == 1, s1, jnp.where(slot == 2, s2, 0.0)))
                    lanes = pl.ds(pl.multiple_of(column * SHARE + p * 128, 128), 128)
                    top = pl.multiple_of(yl * 128 + i * BLK, BLK)
                    h, g = split(t)
                    out[pl.ds(top, BLK), lanes] = h
                    out[pl.ds(pl.multiple_of(ROWS + top, BLK), BLK), lanes] = g


def spread(index, source, pieces, two, hi, lo):
    low = low_half((BLK, 128))
    top = 0
    for piece in pieces:
        v = piece[...]
        n = v.shape[0]
        two[top : top + n, :] = v
        two[HELD + top : HELD + top + n, :] = pltpu.roll(v, BLK, 1)
        top += n
    two[SLABS * BLK : HELD, :] = jnp.zeros((BLK, 128), F32)
    two[HELD + SLABS * BLK :, :] = jnp.zeros((BLK, 128), F32)
    for k in range(KB):
        for p in range(JB // 2):
            s0 = index[source, k * JB + 2 * p]
            s1 = index[source, k * JB + 2 * p + 1]
            r0 = (s0 & 1) * HELD + lax.shift_right_logical(s0, 1) * BLK
            r1 = (1 - (s1 & 1)) * HELD + lax.shift_right_logical(s1, 1) * BLK
            v0 = two[pl.ds(pl.multiple_of(r0, BLK), BLK), :]
            v1 = two[pl.ds(pl.multiple_of(r1, BLK), BLK), :]
            h, g = split(jnp.where(low, v0, v1))
            hi[k * BLK : (k + 1) * BLK, p * 128 : (p + 1) * 128] = h
            lo[k * BLK : (k + 1) * BLK, p * 128 : (p + 1) * 128] = g


def unpack_right(offsets, index, *refs):
    n = len(offsets)
    shares, (hi, lo, two) = refs[:n], refs[n:]
    l, z, y, c = place()
    for t, offset in enumerate(offsets):
        spread(index, (z + offset) % NZ, shares[t : t + 1], two.at[t], hi.at[t], lo.at[t])


def multiply(mine, ready, fresh, first, parted, index, left, *refs):
    refs = list(refs)
    take = lambda n: [refs.pop(0) for _ in range(n)]
    l, z, y, c = place()
    parts = []
    for group in ready:
        hi, lo = take(2)
        parts += [(offset, hi.at[t], lo.at[t]) for t, offset in enumerate(group)]
    shares = [take(n) for _, n in fresh]
    total = None if first else take(1)[0]
    outs = take(2 if parted else 1)
    for t, (offset, _) in enumerate(fresh):
        two, hi, lo = refs
        spread(index, (z + offset) % NZ, shares[t], two.at[t], hi.at[t], lo.at[t])
        parts.append((offset, hi.at[t], lo.at[t]))
    top = (y if mine else 1 - y) * 128
    upper = pl.ds(pl.multiple_of(top, 128), 128)
    lower = pl.ds(pl.multiple_of(ROWS + top, 128), 128)
    dot = functools.partial(jnp.dot, preferred_element_type=F32)

    def columns(cols):
        done = None if first else total[:, cols]
        for offset, hi, lo in parts:
            ks = pl.ds(pl.multiple_of(((z + offset) % NZ) * SHARE, SHARE), SHARE)
            both = jnp.concatenate([left[upper, ks], left[lower, ks]], axis=0)
            big = dot(both, hi[:, cols])
            one = (big[128:] + dot(left[upper, ks], lo[:, cols])) + big[:128]
            done = one if done is None else done + one
        return done

    if parted:
        width = COLS // 2
        for out, start in zip(outs, (l * width, (1 - l) * width)):
            for n0 in range(0, width, 256):
                out[:, n0 : n0 + 256] = columns(pl.ds(pl.multiple_of(start + n0, 256), 256))
    else:
        for n0 in range(0, COLS, 256):
            outs[0][:, n0 : n0 + 256] = columns(slice(n0, n0 + 256))


def call_pack(*args):
    return pl.pallas_call(
        pack,
        out_shape=(
            jax.ShapeDtypeStruct((LPACK, 128), F32),
            jax.ShapeDtypeStruct((SLABS * BLK, 128), F32),
            jax.ShapeDtypeStruct((16, 128), jnp.int32),
        ),
        in_specs=[HBM] * 4,
        out_specs=(VMEM, VMEM, VMEM),
        scratch_shapes=[
            pltpu.VMEM((LI * BLK, LQ * BLK), F32),
            pltpu.VMEM((SHARE, COLS), F32),
            pltpu.SMEM((8, 128), jnp.int32),
            pltpu.SMEM((8, 128), jnp.int32),
            pltpu.SMEM((16,), jnp.int32),
            pltpu.SMEM((16,), jnp.int32),
            pltpu.VMEM((8, 128), jnp.int32),
            pltpu.VMEM((64, 128), jnp.int32),
            pltpu.SemaphoreType.DMA((6,)),
        ],
        compiler_params=ALONE,
        cost_estimate=cost(0, 1 << 20),
    )(*args)


def call_join(parts):
    return pl.pallas_call(
        join,
        out_shape=jax.ShapeDtypeStruct((len(parts) * LPACK, 128), F32),
        in_specs=[VMEM] * len(parts),
        out_specs=VMEM,
        compiler_params=PARAMS,
        cost_estimate=cost(0, 1 << 18),
    )(*parts)


def call_unpack_left(index, lefts):
    return pl.pallas_call(
        unpack_left,
        out_shape=jax.ShapeDtypeStruct((2 * ROWS, NZ * SHARE), BF16),
        in_specs=[SMEM] + [VMEM] * 4,
        out_specs=VMEM,
        compiler_params=PARAMS,
        cost_estimate=cost(0, 1 << 16),
    )(index, *lefts)


def call_unpack_right(offsets, index, shares):
    n = len(offsets)
    return pl.pallas_call(
        functools.partial(unpack_right, offsets),
        out_shape=(jax.ShapeDtypeStruct((n, SHARE, COLS), BF16),) * 2,
        in_specs=[SMEM] + [VMEM] * n,
        out_specs=(VMEM, VMEM),
        scratch_shapes=[pltpu.VMEM((n, 2 * HELD, 128), F32)],
        compiler_params=PARAMS,
        cost_estimate=cost(0, n << 20),
    )(index, *shares)


def call_multiply(mine, index, left, ready, fresh, total=None, parted=False):
    n = len(fresh)
    operands = [array for _, arrays in ready for array in arrays]
    operands += [piece for _, pieces in fresh for piece in pieces]
    operands += [] if total is None else [total]
    shape = jax.ShapeDtypeStruct((128, COLS // 2 if parted else COLS), F32)
    count = n + sum(len(offsets) for offsets, _ in ready)
    kernel = functools.partial(
        multiply,
        mine,
        [offsets for offsets, _ in ready],
        [(offset, len(pieces)) for offset, pieces in fresh],
        total is None,
        parted,
    )
    return pl.pallas_call(
        kernel,
        out_shape=(shape, shape) if parted else shape,
        in_specs=[SMEM] + [VMEM] * (1 + len(operands)),
        out_specs=(VMEM, VMEM) if parted else VMEM,
        scratch_shapes=[
            pltpu.VMEM((n, 2 * HELD, 128), F32),
            pltpu.VMEM((n, SHARE, COLS), BF16),
            pltpu.VMEM((n, SHARE, COLS), BF16),
        ],
        compiler_params=PARAMS,
        cost_estimate=cost(count * 3 * ROWS * SHARE * COLS, 4 * ROWS * COLS),
    )(index, left, *operands)


def z_perm(d):
    return [(z * 2 + y, ((z + d) % NZ) * 2 + y) for z in range(NZ) for y in range(2)]


def x_perm(d):
    return [(((x + d) % 4) * 2 + y, x * 2 + y) for x in range(4) for y in range(2)]


def local(left_tensor, right_tensor, left_occupied, right_occupied):
    l = lax.axis_index("layer")
    left0, right0, index = call_pack(left_tensor, right_tensor, left_occupied, right_occupied)

    pair = [(r, r ^ 1) for r in range(16)]
    near = lambda dy, dh: [(r * 8 + c, (r ^ dy) * 8 + (c ^ dh)) for r in range(16) for c in range(8)]
    z_send = lambda v, d: lax.ppermute(v, "row", z_perm(d))
    up1, down1 = z_send(right0, 1), z_send(right0, -1)
    left2 = call_join(
        [left0]
        + [lax.ppermute(left0, ("row", "col"), near(dy, dh)) for dy, dh in ((1, 0), (0, 1), (1, 1))]
    )
    rights0 = call_unpack_right((0,), index, (right0,))
    up1, down1, left2, rights0 = lax.optimization_barrier((up1, down1, left2, rights0))
    up2, down2 = z_send(up1, 1), z_send(down1, -1)
    x_send = lambda v, d: lax.ppermute(v, "col", x_perm(d))
    lefts = [left2] + [x_send(left2, d) for d in (1, 2, 3)]
    up3, down3 = z_send(up2, 1), z_send(down2, -1)
    near_z = (-1, 1, -2, 2)
    rights = call_unpack_right(near_z, index, (up1, down1, up2, down2))
    ready = [((0,), rights0), (near_z, rights)]
    third = [(-3, (up3,)), (3, (down3,))]
    half = SLABS * BLK // 2
    far = z_send(up3[:half], 1), z_send(down3[half:], -1)

    left = call_unpack_left(index, lefts)
    swap = [(0, 1), (1, 0)]
    total = call_multiply(False, index, left, ready, third)
    keep, give = call_multiply(False, index, left, [], [(4, far)], total, parted=True)
    send = keep + lax.ppermute(give, "layer", swap)
    other = lax.ppermute(send, "row", pair)
    left, send = lax.optimization_barrier((left, send))
    mine = call_multiply(True, index, left, ready, third + [(4, far)])
    mine += lax.ppermute(mine, "layer", swap)
    rest = lax.ppermute(other, "layer", swap)
    return mine + jnp.where(
        l == 0, jnp.concatenate([other, rest], axis=1), jnp.concatenate([rest, other], axis=1)
    )


def solution(mesh):
    placed = (P("row", ("layer", "col")), P(("layer", "row"), "col"), P(), P())
    return jax.shard_map(
        local, mesh=mesh, in_specs=placed, out_specs=P("row", "col"), check_vma=False
    )
```

```python
import functools

import jax
import jax.numpy as jnp
from jax import lax
from jax.experimental import pallas as pl
from jax.experimental.pallas import tpu as pltpu
from jax.sharding import PartitionSpec as P


BLK = 64
KB = 4
JB = 16
LI, LQ = 2, 8
RCAP, LCAP = 12, 3
NZ, NC = 8, 8
SHARE = KB * BLK
COLS = JB * BLK
ROWS = 2 * LI * BLK
SLABS = RCAP // 2
LPACK = 96
F32, BF16 = jnp.float32, jnp.bfloat16
VMEM = pl.BlockSpec(memory_space=pltpu.VMEM)
SMEM = pl.BlockSpec(memory_space=pltpu.SMEM)
HBM = pl.BlockSpec(memory_space=pltpu.HBM)
PARAMS = pltpu.CompilerParams(vmem_limit_bytes=32 * 1024 * 1024)
EMPTY = RCAP
HELD = (SLABS + 1) * BLK


def place():
    r = lax.axis_index("row")
    return lax.axis_index("layer"), r // 2, r % 2, lax.axis_index("col")


def low_half(shape):
    return lax.broadcasted_iota(jnp.int32, shape, 1) < BLK


def cost(flops, moved):
    return pl.CostEstimate(flops=flops, bytes_accessed=moved, transcendentals=0)


def block_at(ref, e, per_row, odd):
    k, j = e // per_row, e % per_row
    v = ref[
        pl.ds(pl.multiple_of(k * BLK, BLK), BLK),
        pl.ds(pl.multiple_of((j // 2) * 128, 128), 128),
    ]
    return jnp.where(j % 2 == odd, v, pltpu.roll(v, BLK, 1))


def ranks(flags, per_row, rows, none):
    n = flags.shape[0]
    f = flags.astype(F32)
    a, b = grid((128, 128))
    same = a // per_row == b // per_row
    in_row = pick(f, same & (a < b))
    row_sum = pick(f, same)
    a, b = grid((n, n))
    before = pick((a // rows == b // rows) & (b < a), row_sum)
    return jnp.where(f > 0, in_row + before, none)


def grid(shape):
    return [lax.broadcasted_iota(jnp.int32, shape, d) for d in (0, 1)]


def pick(a, b):
    return jnp.dot(
        a.astype(F32).astype(BF16), b.astype(F32).astype(BF16), preferred_element_type=F32
    )


def pack(
    left_hbm, right_hbm, left_occupied, right_occupied, left_out, right_out, slots,
    left, right, lflags, rflags, lindex, rindex, lall, rall, sems,
):
    l, z, y, c = place()
    ltop = pl.multiple_of((z // 2) * 8, 8)
    rtop = pl.multiple_of(l * 64 + z * 8, 8)
    ptop = pl.multiple_of(l * 64, 64)
    copies = [
        pltpu.make_async_copy(right_occupied.at[pl.ds(rtop, 8)], rflags, sems.at[0]),
        pltpu.make_async_copy(left_occupied.at[pl.ds(ltop, 8)], lflags, sems.at[1]),
        pltpu.make_async_copy(right_hbm, right, sems.at[2]),
        pltpu.make_async_copy(left_hbm, left, sems.at[3]),
        pltpu.make_async_copy(right_occupied.at[pl.ds(ptop, 64)], rall, sems.at[4]),
        pltpu.make_async_copy(left_occupied.at[pl.ds(ltop, 8)], lall, sems.at[5]),
    ]
    for copy in copies:
        copy.start()
    copies[0].wait()
    rcount = jnp.int32(0)
    for k in range(KB):
        for j in range(JB):
            rindex[rcount] = k * JB + j
            rcount += rflags[y * KB + k, c * JB + j]
    copies[1].wait()
    lcount = jnp.int32(0)
    for i in range(LI):
        for q in range(LQ):
            lindex[lcount] = i * LQ + q
            lcount += lflags[(z % 2) * 4 + y * LI + i, l * 64 + c * LQ + q]
    copies[4].wait()
    copies[5].wait()
    rank = ranks(rall[...], JB, KB, float(EMPTY))
    a, b = grid((8, 64))
    g, h = grid((128, 128))
    total = jnp.zeros((8, 128), F32)
    for k in range(KB):
        row = pick(b == a * 8 + y * KB + k, rank)
        total += pick(row, (h // JB == k) & (g == c * JB + h % JB))
    slots[:8, :] = total.astype(jnp.int32)
    rank = ranks(lall[...], LQ, LI, -1.0)
    a, b = grid((8, 8))
    row = pick(b == (z % 2) * 4 + a, rank)
    row = pick(row, (h < 32) & (g == l * 64 + (h // KB) * LQ + y * KB + h % KB))
    slots[8:, :] = row.astype(jnp.int32)
    low = low_half((BLK, 128))
    copies[2].wait()
    for p in range(SLABS):
        ea = jnp.where(2 * p < rcount, rindex[2 * p], 0)
        eb = jnp.where(2 * p + 1 < rcount, rindex[2 * p + 1], 0)
        right_out[p * BLK : (p + 1) * BLK, :] = jnp.where(
            low, block_at(right, ea, JB, 0), block_at(right, eb, JB, 1)
        )
    copies[3].wait()
    e = [jnp.where(s < lcount, lindex[s], 0) for s in range(LCAP)]
    left_out[:BLK, :] = jnp.where(low, block_at(left, e[0], LQ, 0), block_at(left, e[1], LQ, 1))
    a = block_at(left, e[2], LQ, 0)
    b = block_at(left, e[2], LQ, 1)
    left_out[BLK:, :] = jnp.where(low_half((BLK // 2, 128)), a[: BLK // 2], b[BLK // 2 :])


def join(*refs):
    *parts, out = refs
    for t, part in enumerate(parts):
        out[t * LPACK : (t + 1) * LPACK, :] = part[...]


def split(v):
    h = v.astype(BF16)
    return h, (v - h.astype(F32)).astype(BF16)


def unpack_left(index, a0, a1, a2, a3, out):
    l, z, y, c = place()
    x = c // 2
    low = low_half((BLK, 128))
    low2 = low_half((BLK // 2, 128))
    for d, ref in enumerate((a0, a1, a2, a3)):
        for part in range(4):
            yh = (c % 2) ^ (part // 2)
            yl = y ^ (part % 2)
            column = ((x + d) % 4) * 2 + yh
            base = part * LPACK
            v = ref[base : base + BLK, :]
            w = ref[base + BLK : base + LPACK, :]
            vr, wr = pltpu.roll(v, BLK, 1), pltpu.roll(w, BLK, 1)
            s0 = jnp.where(low, v, vr)
            s1 = jnp.where(low, vr, v)
            s2 = jnp.concatenate([jnp.where(low2, w, wr), jnp.where(low2, wr, w)], axis=0)
            for i in range(LI):
                for p in range(KB // 2):
                    at = column * KB + 2 * p
                    slot = jnp.where(low, index[8 + yl * LI + i, at], index[8 + yl * LI + i, at + 1])
                    t = jnp.where(slot == 0, s0, jnp.where(slot == 1, s1, jnp.where(slot == 2, s2, 0.0)))
                    lanes = pl.ds(pl.multiple_of(column * SHARE + p * 128, 128), 128)
                    top = pl.multiple_of(yl * 128 + i * BLK, BLK)
                    h, g = split(t)
                    out[pl.ds(top, BLK), lanes] = h
                    out[pl.ds(pl.multiple_of(ROWS + top, BLK), BLK), lanes] = g


def spread(index, source, pieces, two, hi, lo):
    low = low_half((BLK, 128))
    top = 0
    for piece in pieces:
        v = piece[...]
        n = v.shape[0]
        two[top : top + n, :] = v
        two[HELD + top : HELD + top + n, :] = pltpu.roll(v, BLK, 1)
        top += n
    two[SLABS * BLK : HELD, :] = jnp.zeros((BLK, 128), F32)
    two[HELD + SLABS * BLK :, :] = jnp.zeros((BLK, 128), F32)
    for k in range(KB):
        for p in range(JB // 2):
            s0 = index[source, k * JB + 2 * p]
            s1 = index[source, k * JB + 2 * p + 1]
            r0 = (s0 & 1) * HELD + lax.shift_right_logical(s0, 1) * BLK
            r1 = (1 - (s1 & 1)) * HELD + lax.shift_right_logical(s1, 1) * BLK
            v0 = two[pl.ds(pl.multiple_of(r0, BLK), BLK), :]
            v1 = two[pl.ds(pl.multiple_of(r1, BLK), BLK), :]
            h, g = split(jnp.where(low, v0, v1))
            hi[k * BLK : (k + 1) * BLK, p * 128 : (p + 1) * 128] = h
            lo[k * BLK : (k + 1) * BLK, p * 128 : (p + 1) * 128] = g


def unpack_right(offsets, index, *refs):
    n = len(offsets)
    shares, (hi, lo, two) = refs[:n], refs[n:]
    l, z, y, c = place()
    for t, offset in enumerate(offsets):
        spread(index, (z + offset) % NZ, shares[t : t + 1], two.at[t], hi.at[t], lo.at[t])


def multiply(mine, ready, fresh, first, parted, index, left, *refs):
    refs = list(refs)
    take = lambda n: [refs.pop(0) for _ in range(n)]
    l, z, y, c = place()
    parts = []
    for group in ready:
        hi, lo = take(2)
        parts += [(offset, hi.at[t], lo.at[t]) for t, offset in enumerate(group)]
    shares = [take(n) for _, n in fresh]
    total = None if first else take(1)[0]
    outs = take(2 if parted else 1)
    for t, (offset, _) in enumerate(fresh):
        two, hi, lo = refs
        spread(index, (z + offset) % NZ, shares[t], two.at[t], hi.at[t], lo.at[t])
        parts.append((offset, hi.at[t], lo.at[t]))
    top = (y if mine else 1 - y) * 128
    upper = pl.ds(pl.multiple_of(top, 128), 128)
    lower = pl.ds(pl.multiple_of(ROWS + top, 128), 128)
    dot = functools.partial(jnp.dot, preferred_element_type=F32)

    def columns(cols):
        done = None if first else total[:, cols]
        for offset, hi, lo in parts:
            ks = pl.ds(pl.multiple_of(((z + offset) % NZ) * SHARE, SHARE), SHARE)
            both = jnp.concatenate([left[upper, ks], left[lower, ks]], axis=0)
            big = dot(both, hi[:, cols])
            one = (big[128:] + dot(left[upper, ks], lo[:, cols])) + big[:128]
            done = one if done is None else done + one
        return done

    if parted:
        width = COLS // 2
        for out, start in zip(outs, (l * width, (1 - l) * width)):
            for n0 in range(0, width, 256):
                out[:, n0 : n0 + 256] = columns(pl.ds(pl.multiple_of(start + n0, 256), 256))
    else:
        for n0 in range(0, COLS, 256):
            outs[0][:, n0 : n0 + 256] = columns(slice(n0, n0 + 256))


def call_pack(*args):
    return pl.pallas_call(
        pack,
        out_shape=(
            jax.ShapeDtypeStruct((LPACK, 128), F32),
            jax.ShapeDtypeStruct((SLABS * BLK, 128), F32),
            jax.ShapeDtypeStruct((16, 128), jnp.int32),
        ),
        in_specs=[HBM] * 4,
        out_specs=(VMEM, VMEM, VMEM),
        scratch_shapes=[
            pltpu.VMEM((LI * BLK, LQ * BLK), F32),
            pltpu.VMEM((SHARE, COLS), F32),
            pltpu.SMEM((8, 128), jnp.int32),
            pltpu.SMEM((8, 128), jnp.int32),
            pltpu.SMEM((16,), jnp.int32),
            pltpu.SMEM((16,), jnp.int32),
            pltpu.VMEM((8, 128), jnp.int32),
            pltpu.VMEM((64, 128), jnp.int32),
            pltpu.SemaphoreType.DMA((6,)),
        ],
        compiler_params=PARAMS,
        cost_estimate=cost(0, 1 << 20),
    )(*(pltpu.with_memory_space_constraint(a, pltpu.HBM) for a in args))


def call_join(parts):
    return pl.pallas_call(
        join,
        out_shape=jax.ShapeDtypeStruct((len(parts) * LPACK, 128), F32),
        in_specs=[VMEM] * len(parts),
        out_specs=VMEM,
        compiler_params=PARAMS,
        cost_estimate=cost(0, 1 << 18),
    )(*parts)


def call_unpack_left(index, lefts):
    return pl.pallas_call(
        unpack_left,
        out_shape=jax.ShapeDtypeStruct((2 * ROWS, NZ * SHARE), BF16),
        in_specs=[SMEM] + [VMEM] * 4,
        out_specs=VMEM,
        compiler_params=PARAMS,
        cost_estimate=cost(0, 1 << 16),
    )(index, *lefts)


def call_unpack_right(offsets, index, shares):
    n = len(offsets)
    return pl.pallas_call(
        functools.partial(unpack_right, offsets),
        out_shape=(jax.ShapeDtypeStruct((n, SHARE, COLS), BF16),) * 2,
        in_specs=[SMEM] + [VMEM] * n,
        out_specs=(VMEM, VMEM),
        scratch_shapes=[pltpu.VMEM((n, 2 * HELD, 128), F32)],
        compiler_params=PARAMS,
        cost_estimate=cost(0, n << 20),
    )(index, *shares)


def call_multiply(mine, index, left, ready, fresh, total=None, parted=False):
    n = len(fresh)
    operands = [array for _, arrays in ready for array in arrays]
    operands += [piece for _, pieces in fresh for piece in pieces]
    operands += [] if total is None else [total]
    shape = jax.ShapeDtypeStruct((128, COLS // 2 if parted else COLS), F32)
    count = n + sum(len(offsets) for offsets, _ in ready)
    kernel = functools.partial(
        multiply,
        mine,
        [offsets for offsets, _ in ready],
        [(offset, len(pieces)) for offset, pieces in fresh],
        total is None,
        parted,
    )
    return pl.pallas_call(
        kernel,
        out_shape=(shape, shape) if parted else shape,
        in_specs=[SMEM] + [VMEM] * (1 + len(operands)),
        out_specs=(VMEM, VMEM) if parted else VMEM,
        scratch_shapes=[
            pltpu.VMEM((n, 2 * HELD, 128), F32),
            pltpu.VMEM((n, SHARE, COLS), BF16),
            pltpu.VMEM((n, SHARE, COLS), BF16),
        ],
        compiler_params=PARAMS,
        cost_estimate=cost(count * 3 * ROWS * SHARE * COLS, 4 * ROWS * COLS),
    )(index, left, *operands)


def z_perm(d):
    return [(z * 2 + y, ((z + d) % NZ) * 2 + y) for z in range(NZ) for y in range(2)]


def x_perm(d):
    return [(((x + d) % 4) * 2 + y, x * 2 + y) for x in range(4) for y in range(2)]


def local(left_tensor, right_tensor, left_occupied, right_occupied):
    l = lax.axis_index("layer")
    left0, right0, index = call_pack(left_tensor, right_tensor, left_occupied, right_occupied)

    pair = [(r, r ^ 1) for r in range(16)]
    near = lambda dy, dh: [(r * 8 + c, (r ^ dy) * 8 + (c ^ dh)) for r in range(16) for c in range(8)]
    z_send = lambda v, d: lax.ppermute(v, "row", z_perm(d))
    up1, down1 = z_send(right0, 1), z_send(right0, -1)
    nears = [lax.ppermute(left0, ("row", "col"), near(dy, dh)) for dy, dh in ((1, 0), (0, 1), (1, 1))]
    rights0 = call_unpack_right((0,), index, (right0,))
    up1, down1, rights0, *nears = lax.optimization_barrier((up1, down1, rights0, *nears))
    left2 = call_join([left0] + nears)
    up2, down2 = z_send(up1, 1), z_send(down1, -1)
    x_send = lambda v, d: lax.ppermute(v, "col", x_perm(d))
    lefts = [left2] + [x_send(left2, d) for d in (1, 2, 3)]
    up3, down3 = z_send(up2, 1), z_send(down2, -1)
    near_z = (-1, 1, -2, 2)
    rights = call_unpack_right(near_z, index, (up1, down1, up2, down2))
    ready = [((0,), rights0), (near_z, rights)]
    third = [(-3, (up3,)), (3, (down3,))]
    half = SLABS * BLK // 2
    far = z_send(up3[:half], 1), z_send(down3[half:], -1)

    left = call_unpack_left(index, lefts)
    swap = [(0, 1), (1, 0)]
    total = call_multiply(False, index, left, ready, third)
    keep, give = call_multiply(False, index, left, [], [(4, far)], total, parted=True)
    send = keep + lax.ppermute(give, "layer", swap)
    other = lax.ppermute(send, "row", pair)
    left, send = lax.optimization_barrier((left, send))
    mine = call_multiply(True, index, left, ready, third + [(4, far)])
    mine += lax.ppermute(mine, "layer", swap)
    rest = lax.ppermute(other, "layer", swap)
    return mine + jnp.where(
        l == 0, jnp.concatenate([other, rest], axis=1), jnp.concatenate([rest, other], axis=1)
    )


def solution(mesh):
    placed = (P("row", ("layer", "col")), P(("layer", "row"), "col"), P(), P())
    return jax.shard_map(
        local, mesh=mesh, in_specs=placed, out_specs=P("row", "col"), check_vma=False
    )
```

```python
import functools

import jax
import jax.numpy as jnp
from jax import lax
from jax.experimental import pallas as pl
from jax.experimental.pallas import tpu as pltpu
from jax.sharding import PartitionSpec as P


BLK = 64
KB = 4
JB = 16
LI, LQ = 2, 8
RCAP, LCAP = 12, 3
NZ, NC = 8, 8
SHARE = KB * BLK
COLS = JB * BLK
ROWS = 2 * LI * BLK
SLABS = RCAP // 2
LPACK = 96
F32, BF16 = jnp.float32, jnp.bfloat16
VMEM = pl.BlockSpec(memory_space=pltpu.VMEM)
SMEM = pl.BlockSpec(memory_space=pltpu.SMEM)
HBM = pl.BlockSpec(memory_space=pltpu.HBM)
PARAMS = pltpu.CompilerParams(vmem_limit_bytes=32 * 1024 * 1024)
EMPTY = RCAP
HELD = (SLABS + 1) * BLK


def place():
    r = lax.axis_index("row")
    return lax.axis_index("layer"), r // 2, r % 2, lax.axis_index("col")


def low_half(shape):
    return lax.broadcasted_iota(jnp.int32, shape, 1) < BLK


def cost(flops, moved):
    return pl.CostEstimate(flops=flops, bytes_accessed=moved, transcendentals=0)


def block_at(ref, e, per_row, odd):
    k, j = e // per_row, e % per_row
    v = ref[
        pl.ds(pl.multiple_of(k * BLK, BLK), BLK),
        pl.ds(pl.multiple_of((j // 2) * 128, 128), 128),
    ]
    return jnp.where(j % 2 == odd, v, pltpu.roll(v, BLK, 1))


def ranks(flags, per_row, rows, none):
    n = flags.shape[0]
    f = flags.astype(F32)
    a, b = grid((128, 128))
    same = a // per_row == b // per_row
    in_row = pick(f, same & (a < b))
    row_sum = pick(f, same)
    a, b = grid((n, n))
    before = pick((a // rows == b // rows) & (b < a), row_sum)
    return jnp.where(f > 0, in_row + before, none)


def grid(shape):
    return [lax.broadcasted_iota(jnp.int32, shape, d) for d in (0, 1)]


def pick(a, b):
    return jnp.dot(
        a.astype(F32).astype(BF16), b.astype(F32).astype(BF16), preferred_element_type=F32
    )


def pack(
    left_hbm, right_hbm, left_occupied, right_occupied, left_out, right_out,
    left, right, lflags, rflags, lindex, rindex, sems,
):
    l, z, y, c = place()
    ltop = pl.multiple_of((z // 2) * 8, 8)
    rtop = pl.multiple_of(l * 64 + z * 8, 8)
    copies = [
        pltpu.make_async_copy(right_occupied.at[pl.ds(rtop, 8)], rflags, sems.at[0]),
        pltpu.make_async_copy(left_occupied.at[pl.ds(ltop, 8)], lflags, sems.at[1]),
        pltpu.make_async_copy(right_hbm, right, sems.at[2]),
        pltpu.make_async_copy(left_hbm, left, sems.at[3]),
    ]
    for copy in copies:
        copy.start()
    copies[0].wait()
    rcount = jnp.int32(0)
    for k in range(KB):
        for j in range(JB):
            rindex[rcount] = k * JB + j
            rcount += rflags[y * KB + k, c * JB + j]
    copies[1].wait()
    lcount = jnp.int32(0)
    for i in range(LI):
        for q in range(LQ):
            lindex[lcount] = i * LQ + q
            lcount += lflags[(z % 2) * 4 + y * LI + i, l * 64 + c * LQ + q]
    low = low_half((BLK, 128))
    copies[2].wait()
    for p in range(SLABS):
        ea = jnp.where(2 * p < rcount, rindex[2 * p], 0)
        eb = jnp.where(2 * p + 1 < rcount, rindex[2 * p + 1], 0)
        right_out[p * BLK : (p + 1) * BLK, :] = jnp.where(
            low, block_at(right, ea, JB, 0), block_at(right, eb, JB, 1)
        )
    copies[3].wait()
    e = [jnp.where(s < lcount, lindex[s], 0) for s in range(LCAP)]
    left_out[:BLK, :] = jnp.where(low, block_at(left, e[0], LQ, 0), block_at(left, e[1], LQ, 1))
    a = block_at(left, e[2], LQ, 0)
    b = block_at(left, e[2], LQ, 1)
    left_out[BLK:, :] = jnp.where(low_half((BLK // 2, 128)), a[: BLK // 2], b[BLK // 2 :])


def tables(left_occupied, right_occupied, slots, lall, rall, sems):
    l, z, y, c = place()
    ltop = pl.multiple_of((z // 2) * 8, 8)
    ptop = pl.multiple_of(l * 64, 64)
    copies = [
        pltpu.make_async_copy(right_occupied.at[pl.ds(ptop, 64)], rall, sems.at[0]),
        pltpu.make_async_copy(left_occupied.at[pl.ds(ltop, 8)], lall, sems.at[1]),
    ]
    for copy in copies:
        copy.start()
    for copy in copies:
        copy.wait()
    rank = ranks(rall[...], JB, KB, float(EMPTY))
    a, b = grid((8, 64))
    g, h = grid((128, 128))
    total = jnp.zeros((8, 128), F32)
    for k in range(KB):
        row = pick(b == a * 8 + y * KB + k, rank)
        total += pick(row, (h // JB == k) & (g == c * JB + h % JB))
    slots[:8, :] = total.astype(jnp.int32)
    rank = ranks(lall[...], LQ, LI, -1.0)
    a, b = grid((8, 8))
    row = pick(b == (z % 2) * 4 + a, rank)
    row = pick(row, (h < 32) & (g == l * 64 + (h // KB) * LQ + y * KB + h % KB))
    slots[8:, :] = row.astype(jnp.int32)


def join(*refs):
    *parts, out = refs
    for t, part in enumerate(parts):
        out[t * LPACK : (t + 1) * LPACK, :] = part[...]


def split(v):
    h = v.astype(BF16)
    return h, (v - h.astype(F32)).astype(BF16)


def unpack_left(index, a0, a1, a2, a3, out):
    l, z, y, c = place()
    x = c // 2
    low = low_half((BLK, 128))
    low2 = low_half((BLK // 2, 128))
    for d, ref in enumerate((a0, a1, a2, a3)):
        for part in range(4):
            yh = (c % 2) ^ (part // 2)
            yl = y ^ (part % 2)
            column = ((x + d) % 4) * 2 + yh
            base = part * LPACK
            v = ref[base : base + BLK, :]
            w = ref[base + BLK : base + LPACK, :]
            vr, wr = pltpu.roll(v, BLK, 1), pltpu.roll(w, BLK, 1)
            s0 = jnp.where(low, v, vr)
            s1 = jnp.where(low, vr, v)
            s2 = jnp.concatenate([jnp.where(low2, w, wr), jnp.where(low2, wr, w)], axis=0)
            for i in range(LI):
                for p in range(KB // 2):
                    at = column * KB + 2 * p
                    slot = jnp.where(low, index[8 + yl * LI + i, at], index[8 + yl * LI + i, at + 1])
                    t = jnp.where(slot == 0, s0, jnp.where(slot == 1, s1, jnp.where(slot == 2, s2, 0.0)))
                    lanes = pl.ds(pl.multiple_of(column * SHARE + p * 128, 128), 128)
                    top = pl.multiple_of(yl * 128 + i * BLK, BLK)
                    h, g = split(t)
                    out[pl.ds(top, BLK), lanes] = h
                    out[pl.ds(pl.multiple_of(ROWS + top, BLK), BLK), lanes] = g


def spread(index, source, pieces, two, hi, lo, first=0):
    low = low_half((BLK, 128))
    top = 0
    for piece in pieces:
        v = piece[...]
        n = v.shape[0]
        two[top : top + n, :] = v
        two[HELD + top : HELD + top + n, :] = pltpu.roll(v, BLK, 1)
        top += n
    two[SLABS * BLK : HELD, :] = jnp.zeros((BLK, 128), F32)
    two[HELD + SLABS * BLK :, :] = jnp.zeros((BLK, 128), F32)
    for k in range(KB):
        for p in range(hi.shape[1] // 128):
            s0 = index[source, k * JB + 2 * (first + p)]
            s1 = index[source, k * JB + 2 * (first + p) + 1]
            r0 = (s0 & 1) * HELD + lax.shift_right_logical(s0, 1) * BLK
            r1 = (1 - (s1 & 1)) * HELD + lax.shift_right_logical(s1, 1) * BLK
            v0 = two[pl.ds(pl.multiple_of(r0, BLK), BLK), :]
            v1 = two[pl.ds(pl.multiple_of(r1, BLK), BLK), :]
            h, g = split(jnp.where(low, v0, v1))
            hi[k * BLK : (k + 1) * BLK, p * 128 : (p + 1) * 128] = h
            lo[k * BLK : (k + 1) * BLK, p * 128 : (p + 1) * 128] = g


def unpack_right(offsets, index, *refs):
    n = len(offsets)
    shares, (hi, lo, two) = refs[:n], refs[n:]
    l, z, y, c = place()
    for t, offset in enumerate(offsets):
        spread(index, (z + offset) % NZ, shares[t : t + 1], two.at[t], hi.at[t], lo.at[t])


def row_parts(left, mine, y):
    top = (y if mine else 1 - y) * 128
    upper = pl.ds(pl.multiple_of(top, 128), 128)
    lower = pl.ds(pl.multiple_of(ROWS + top, 128), 128)
    return lambda ks: (left[upper, ks], left[lower, ks])


def product(parts, hi, lo):
    dot = functools.partial(jnp.dot, preferred_element_type=F32)
    big = dot(jnp.concatenate(parts, axis=0), hi)
    return (big[128:] + dot(parts[0], lo)) + big[:128]


def finish(offset, keep, index, left, share0, share1, total, out, two, hi, lo):
    l, z, y, c = place()
    source = (z + offset) % NZ
    half = l if keep else 1 - l
    spread(index, source, (share0, share1), two, hi, lo, half * (JB // 4))
    parts = row_parts(left, False, y)(pl.ds(pl.multiple_of(source * SHARE, SHARE), SHARE))
    width = COLS // 2
    for n0 in range(0, width, 256):
        cols = pl.ds(pl.multiple_of(half * width + n0, 256), 256)
        out[:, n0 : n0 + 256] = total[:, cols] + product(
            parts, hi[:, n0 : n0 + 256], lo[:, n0 : n0 + 256]
        )


def multiply(mine, ready, fresh, index, left, *refs):
    refs = list(refs)
    take = lambda n: [refs.pop(0) for _ in range(n)]
    l, z, y, c = place()
    parts = []
    for group in ready:
        hi, lo = take(2)
        parts += [(offset, hi.at[t], lo.at[t]) for t, offset in enumerate(group)]
    shares = [take(n) for _, n in fresh]
    out, two, hi, lo = refs
    for t, (offset, _) in enumerate(fresh):
        spread(index, (z + offset) % NZ, shares[t], two.at[t], hi.at[t], lo.at[t])
        parts.append((offset, hi.at[t], lo.at[t]))
    rows = row_parts(left, mine, y)
    for n0 in range(0, COLS, 256):
        cols = slice(n0, n0 + 256)
        done = None
        for offset, h, g in parts:
            ks = pl.ds(pl.multiple_of(((z + offset) % NZ) * SHARE, SHARE), SHARE)
            one = product(rows(ks), h[:, cols], g[:, cols])
            done = one if done is None else done + one
        out[:, cols] = done


def in_hbm(arrays):
    return [pltpu.with_memory_space_constraint(a, pltpu.HBM) for a in arrays]


def call_pack(*args):
    return pl.pallas_call(
        pack,
        out_shape=(
            jax.ShapeDtypeStruct((LPACK, 128), F32),
            jax.ShapeDtypeStruct((SLABS * BLK, 128), F32),
        ),
        in_specs=[HBM] * 4,
        out_specs=(VMEM, VMEM),
        scratch_shapes=[
            pltpu.VMEM((LI * BLK, LQ * BLK), F32),
            pltpu.VMEM((SHARE, COLS), F32),
            pltpu.SMEM((8, 128), jnp.int32),
            pltpu.SMEM((8, 128), jnp.int32),
            pltpu.SMEM((16,), jnp.int32),
            pltpu.SMEM((16,), jnp.int32),
            pltpu.SemaphoreType.DMA((4,)),
        ],
        compiler_params=PARAMS,
        cost_estimate=cost(0, 1 << 20),
    )(*in_hbm(args))


def call_tables(*args):
    return pl.pallas_call(
        tables,
        out_shape=jax.ShapeDtypeStruct((16, 128), jnp.int32),
        in_specs=[HBM] * 2,
        out_specs=VMEM,
        scratch_shapes=[
            pltpu.VMEM((8, 128), jnp.int32),
            pltpu.VMEM((64, 128), jnp.int32),
            pltpu.SemaphoreType.DMA((2,)),
        ],
        compiler_params=PARAMS,
        cost_estimate=cost(0, 1 << 18),
    )(*in_hbm(args))


def call_join(parts):
    return pl.pallas_call(
        join,
        out_shape=jax.ShapeDtypeStruct((len(parts) * LPACK, 128), F32),
        in_specs=[VMEM] * len(parts),
        out_specs=VMEM,
        compiler_params=PARAMS,
        cost_estimate=cost(0, 1 << 18),
    )(*parts)


def call_unpack_left(index, lefts):
    return pl.pallas_call(
        unpack_left,
        out_shape=jax.ShapeDtypeStruct((2 * ROWS, NZ * SHARE), BF16),
        in_specs=[SMEM] + [VMEM] * 4,
        out_specs=VMEM,
        compiler_params=PARAMS,
        cost_estimate=cost(0, 1 << 16),
    )(index, *lefts)


def call_unpack_right(offsets, index, shares):
    n = len(offsets)
    return pl.pallas_call(
        functools.partial(unpack_right, offsets),
        out_shape=(jax.ShapeDtypeStruct((n, SHARE, COLS), BF16),) * 2,
        in_specs=[SMEM] + [VMEM] * n,
        out_specs=(VMEM, VMEM),
        scratch_shapes=[pltpu.VMEM((n, 2 * HELD, 128), F32)],
        compiler_params=PARAMS,
        cost_estimate=cost(0, n << 20),
    )(index, *shares)


def call_multiply(mine, index, left, ready, fresh):
    n = len(fresh)
    operands = [array for _, arrays in ready for array in arrays]
    operands += [piece for _, pieces in fresh for piece in pieces]
    count = n + sum(len(offsets) for offsets, _ in ready)
    kernel = functools.partial(
        multiply,
        mine,
        [offsets for offsets, _ in ready],
        [(offset, len(pieces)) for offset, pieces in fresh],
    )
    return pl.pallas_call(
        kernel,
        out_shape=jax.ShapeDtypeStruct((128, COLS), F32),
        in_specs=[SMEM] + [VMEM] * (1 + len(operands)),
        out_specs=VMEM,
        scratch_shapes=[
            pltpu.VMEM((n, 2 * HELD, 128), F32),
            pltpu.VMEM((n, SHARE, COLS), BF16),
            pltpu.VMEM((n, SHARE, COLS), BF16),
        ],
        compiler_params=PARAMS,
        cost_estimate=cost(count * 3 * ROWS * SHARE * COLS, 4 * ROWS * COLS),
    )(index, left, *operands)


def call_finish(offset, keep, index, left, pieces, total):
    width = COLS // 2
    return pl.pallas_call(
        functools.partial(finish, offset, keep),
        out_shape=jax.ShapeDtypeStruct((128, width), F32),
        in_specs=[SMEM] + [VMEM] * 4,
        out_specs=VMEM,
        scratch_shapes=[
            pltpu.VMEM((2 * HELD, 128), F32),
            pltpu.VMEM((SHARE, width), BF16),
            pltpu.VMEM((SHARE, width), BF16),
        ],
        compiler_params=PARAMS,
        cost_estimate=cost(3 * 128 * SHARE * COLS, ROWS * COLS),
    )(index, left, *pieces, total)


def z_perm(d):
    return [(z * 2 + y, ((z + d) % NZ) * 2 + y) for z in range(NZ) for y in range(2)]


def x_perm(d):
    return [(((x + d) % 4) * 2 + y, x * 2 + y) for x in range(4) for y in range(2)]


def local(left_tensor, right_tensor, left_occupied, right_occupied):
    l = lax.axis_index("layer")
    left0, right0 = call_pack(left_tensor, right_tensor, left_occupied, right_occupied)
    index = call_tables(left_occupied, right_occupied)

    pair = [(r, r ^ 1) for r in range(16)]
    near = lambda dy, dh: [(r * 8 + c, (r ^ dy) * 8 + (c ^ dh)) for r in range(16) for c in range(8)]
    z_send = lambda v, d: lax.ppermute(v, "row", z_perm(d))
    up1, down1 = z_send(right0, 1), z_send(right0, -1)
    nears = [lax.ppermute(left0, ("row", "col"), near(dy, dh)) for dy, dh in ((1, 0), (0, 1), (1, 1))]
    rights0 = call_unpack_right((0,), index, (right0,))
    up1, down1, rights0, *nears = lax.optimization_barrier((up1, down1, rights0, *nears))
    left2 = call_join([left0] + nears)
    up2, down2 = z_send(up1, 1), z_send(down1, -1)
    x_send = lambda v, d: lax.ppermute(v, "col", x_perm(d))
    lefts = [left2] + [x_send(left2, d) for d in (1, 2, 3)]
    up3, down3 = z_send(up2, 1), z_send(down2, -1)
    near_z = (-1, 1, -2, 2)
    rights = call_unpack_right(near_z, index, (up1, down1, up2, down2))
    ready = [((0,), rights0), (near_z, rights)]
    third = [(-3, (up3,)), (3, (down3,))]
    half = SLABS * BLK // 2
    far = z_send(up3[:half], 1), z_send(down3[half:], -1)

    left = call_unpack_left(index, lefts)
    swap = [(0, 1), (1, 0)]
    total = call_multiply(False, index, left, ready, third)
    give = call_finish(4, False, index, left, far, total)
    recv = lax.ppermute(give, "layer", swap)
    keep = call_finish(4, True, index, left, far, total)
    send = keep + recv
    other = lax.ppermute(send, "row", pair)
    left, send = lax.optimization_barrier((left, send))
    mine = call_multiply(True, index, left, ready, third + [(4, far)])
    mine += lax.ppermute(mine, "layer", swap)
    rest = lax.ppermute(other, "layer", swap)
    return mine + jnp.where(
        l == 0, jnp.concatenate([other, rest], axis=1), jnp.concatenate([rest, other], axis=1)
    )


def solution(mesh):
    placed = (P("row", ("layer", "col")), P(("layer", "row"), "col"), P(), P())
    return jax.shard_map(
        local, mesh=mesh, in_specs=placed, out_specs=P("row", "col"), check_vma=False
    )
```

```python
import functools

import jax
import jax.numpy as jnp
from jax import lax
from jax.experimental import pallas as pl
from jax.experimental.pallas import tpu as pltpu
from jax.sharding import PartitionSpec as P


BLK = 64
KB = 4
JB = 16
LI, LQ = 2, 8
RCAP, LCAP = 12, 3
NZ, NC = 8, 8
SHARE = KB * BLK
COLS = JB * BLK
ROWS = 2 * LI * BLK
SLABS = RCAP // 2
LPACK = 96
F32, BF16 = jnp.float32, jnp.bfloat16
VMEM = pl.BlockSpec(memory_space=pltpu.VMEM)
SMEM = pl.BlockSpec(memory_space=pltpu.SMEM)
HBM = pl.BlockSpec(memory_space=pltpu.HBM)
PARAMS = pltpu.CompilerParams(vmem_limit_bytes=32 * 1024 * 1024)
EMPTY = RCAP
HELD = (SLABS + 1) * BLK


def place():
    r = lax.axis_index("row")
    return lax.axis_index("layer"), r // 2, r % 2, lax.axis_index("col")


def low_half(shape):
    return lax.broadcasted_iota(jnp.int32, shape, 1) < BLK


def cost(flops, moved):
    return pl.CostEstimate(flops=flops, bytes_accessed=moved, transcendentals=0)


def block_at(ref, e, per_row, odd):
    k, j = e // per_row, e % per_row
    v = ref[
        pl.ds(pl.multiple_of(k * BLK, BLK), BLK),
        pl.ds(pl.multiple_of((j // 2) * 128, 128), 128),
    ]
    return jnp.where(j % 2 == odd, v, pltpu.roll(v, BLK, 1))


def ranks(flags, per_row, rows, none):
    n = flags.shape[0]
    f = flags.astype(F32)
    a, b = grid((128, 128))
    same = a // per_row == b // per_row
    in_row = pick(f, same & (a < b))
    row_sum = pick(f, same)
    a, b = grid((n, n))
    before = pick((a // rows == b // rows) & (b < a), row_sum)
    return jnp.where(f > 0, in_row + before, none)


def grid(shape):
    return [lax.broadcasted_iota(jnp.int32, shape, d) for d in (0, 1)]


def pick(a, b):
    return jnp.dot(
        a.astype(F32).astype(BF16), b.astype(F32).astype(BF16), preferred_element_type=F32
    )


def pack(
    left_hbm, right_hbm, left_occupied, right_occupied, left_out, right_out,
    left, right, lflags, rflags, lindex, rindex, sems,
):
    l, z, y, c = place()
    ltop = pl.multiple_of((z // 2) * 8, 8)
    rtop = pl.multiple_of(l * 64 + z * 8, 8)
    copies = [
        pltpu.make_async_copy(right_occupied.at[pl.ds(rtop, 8)], rflags, sems.at[0]),
        pltpu.make_async_copy(left_occupied.at[pl.ds(ltop, 8)], lflags, sems.at[1]),
        pltpu.make_async_copy(right_hbm, right, sems.at[2]),
        pltpu.make_async_copy(left_hbm, left, sems.at[3]),
    ]
    for copy in copies:
        copy.start()
    copies[0].wait()
    rcount = jnp.int32(0)
    for k in range(KB):
        for j in range(JB):
            rindex[rcount] = k * JB + j
            rcount += rflags[y * KB + k, c * JB + j]
    copies[1].wait()
    lcount = jnp.int32(0)
    for i in range(LI):
        for q in range(LQ):
            lindex[lcount] = i * LQ + q
            lcount += lflags[(z % 2) * 4 + y * LI + i, l * 64 + c * LQ + q]
    low = low_half((BLK, 128))
    copies[2].wait()
    for p in range(SLABS):
        ea = jnp.where(2 * p < rcount, rindex[2 * p], 0)
        eb = jnp.where(2 * p + 1 < rcount, rindex[2 * p + 1], 0)
        right_out[p * BLK : (p + 1) * BLK, :] = jnp.where(
            low, block_at(right, ea, JB, 0), block_at(right, eb, JB, 1)
        )
    copies[3].wait()
    e = [jnp.where(s < lcount, lindex[s], 0) for s in range(LCAP)]
    left_out[:BLK, :] = jnp.where(low, block_at(left, e[0], LQ, 0), block_at(left, e[1], LQ, 1))
    a = block_at(left, e[2], LQ, 0)
    b = block_at(left, e[2], LQ, 1)
    left_out[BLK:, :] = jnp.where(low_half((BLK // 2, 128)), a[: BLK // 2], b[BLK // 2 :])


def tables(left_occupied, right_occupied, slots, lall, rall, sems):
    l, z, y, c = place()
    ltop = pl.multiple_of((z // 2) * 8, 8)
    ptop = pl.multiple_of(l * 64, 64)
    copies = [
        pltpu.make_async_copy(right_occupied.at[pl.ds(ptop, 64)], rall, sems.at[0]),
        pltpu.make_async_copy(left_occupied.at[pl.ds(ltop, 8)], lall, sems.at[1]),
    ]
    for copy in copies:
        copy.start()
    for copy in copies:
        copy.wait()
    rank = ranks(rall[...], JB, KB, float(EMPTY))
    a, b = grid((8, 64))
    g, h = grid((128, 128))
    total = jnp.zeros((8, 128), F32)
    for k in range(KB):
        row = pick(b == a * 8 + y * KB + k, rank)
        total += pick(row, (h // JB == k) & (g == c * JB + h % JB))
    slots[:8, :] = total.astype(jnp.int32)
    rank = ranks(lall[...], LQ, LI, -1.0)
    a, b = grid((8, 8))
    row = pick(b == (z % 2) * 4 + a, rank)
    row = pick(row, (h < 32) & (g == l * 64 + (h // KB) * LQ + y * KB + h % KB))
    slots[8:, :] = row.astype(jnp.int32)


def join(*refs):
    *parts, out = refs
    for t, part in enumerate(parts):
        out[t * LPACK : (t + 1) * LPACK, :] = part[...]


def split(v):
    h = v.astype(BF16)
    return h, (v - h.astype(F32)).astype(BF16)


def unpack_left(mine, index, a0, a1, a2, a3, out):
    l, z, y, c = place()
    x = c // 2
    low = low_half((BLK, 128))
    low2 = low_half((BLK // 2, 128))
    for d, ref in enumerate((a0, a1, a2, a3)):
        for part in (0, 2) if mine else (1, 3):
            yh = (c % 2) ^ (part // 2)
            yl = y ^ (part % 2)
            column = ((x + d) % 4) * 2 + yh
            base = part * LPACK
            v = ref[base : base + BLK, :]
            w = ref[base + BLK : base + LPACK, :]
            vr, wr = pltpu.roll(v, BLK, 1), pltpu.roll(w, BLK, 1)
            s0 = jnp.where(low, v, vr)
            s1 = jnp.where(low, vr, v)
            s2 = jnp.concatenate([jnp.where(low2, w, wr), jnp.where(low2, wr, w)], axis=0)
            for i in range(LI):
                for p in range(KB // 2):
                    at = column * KB + 2 * p
                    slot = jnp.where(low, index[8 + yl * LI + i, at], index[8 + yl * LI + i, at + 1])
                    t = jnp.where(slot == 0, s0, jnp.where(slot == 1, s1, jnp.where(slot == 2, s2, 0.0)))
                    lanes = pl.ds(pl.multiple_of(column * SHARE + p * 128, 128), 128)
                    h, g = split(t)
                    out[i * BLK : (i + 1) * BLK, lanes] = h
                    out[128 + i * BLK : 128 + (i + 1) * BLK, lanes] = g


def spread(index, source, pieces, two, hi, lo, first=0):
    low = low_half((BLK, 128))
    top = 0
    for piece in pieces:
        v = piece[...]
        n = v.shape[0]
        two[top : top + n, :] = v
        two[HELD + top : HELD + top + n, :] = pltpu.roll(v, BLK, 1)
        top += n
    two[SLABS * BLK : HELD, :] = jnp.zeros((BLK, 128), F32)
    two[HELD + SLABS * BLK :, :] = jnp.zeros((BLK, 128), F32)
    for k in range(KB):
        for p in range(hi.shape[1] // 128):
            s0 = index[source, k * JB + 2 * (first + p)]
            s1 = index[source, k * JB + 2 * (first + p) + 1]
            r0 = (s0 & 1) * HELD + lax.shift_right_logical(s0, 1) * BLK
            r1 = (1 - (s1 & 1)) * HELD + lax.shift_right_logical(s1, 1) * BLK
            v0 = two[pl.ds(pl.multiple_of(r0, BLK), BLK), :]
            v1 = two[pl.ds(pl.multiple_of(r1, BLK), BLK), :]
            h, g = split(jnp.where(low, v0, v1))
            hi[k * BLK : (k + 1) * BLK, p * 128 : (p + 1) * 128] = h
            lo[k * BLK : (k + 1) * BLK, p * 128 : (p + 1) * 128] = g


def unpack_right(offsets, index, *refs):
    n = len(offsets)
    shares, (hi, lo, two) = refs[:n], refs[n:]
    l, z, y, c = place()
    for t, offset in enumerate(offsets):
        spread(index, (z + offset) % NZ, shares[t : t + 1], two.at[t], hi.at[t], lo.at[t])


def product(left, ks, hi, lo):
    dot = functools.partial(jnp.dot, preferred_element_type=F32)
    big = dot(left[:, ks], hi)
    return (big[128:] + dot(left[:128, ks], lo)) + big[:128]


def finish(offset, keep, index, left, share0, share1, total, out, two, hi, lo):
    l, z, y, c = place()
    source = (z + offset) % NZ
    half = l if keep else 1 - l
    spread(index, source, (share0, share1), two, hi, lo, half * (JB // 4))
    ks = pl.ds(pl.multiple_of(source * SHARE, SHARE), SHARE)
    width = COLS // 2
    for n0 in range(0, width, 256):
        cols = pl.ds(pl.multiple_of(half * width + n0, 256), 256)
        out[:, n0 : n0 + 256] = total[:, cols] + product(
            left, ks, hi[:, n0 : n0 + 256], lo[:, n0 : n0 + 256]
        )


def multiply(ready, fresh, index, left, *refs):
    refs = list(refs)
    take = lambda n: [refs.pop(0) for _ in range(n)]
    l, z, y, c = place()
    parts = []
    for group in ready:
        hi, lo = take(2)
        parts += [(offset, hi.at[t], lo.at[t]) for t, offset in enumerate(group)]
    shares = [take(n) for _, n in fresh]
    out, two, hi, lo = refs
    for t, (offset, _) in enumerate(fresh):
        spread(index, (z + offset) % NZ, shares[t], two.at[t], hi.at[t], lo.at[t])
        parts.append((offset, hi.at[t], lo.at[t]))
    for n0 in range(0, COLS, 256):
        cols = slice(n0, n0 + 256)
        done = None
        for offset, h, g in parts:
            ks = pl.ds(pl.multiple_of(((z + offset) % NZ) * SHARE, SHARE), SHARE)
            one = product(left, ks, h[:, cols], g[:, cols])
            done = one if done is None else done + one
        out[:, cols] = done


def in_hbm(arrays):
    return [pltpu.with_memory_space_constraint(a, pltpu.HBM) for a in arrays]


def call_pack(*args):
    return pl.pallas_call(
        pack,
        out_shape=(
            jax.ShapeDtypeStruct((LPACK, 128), F32),
            jax.ShapeDtypeStruct((SLABS * BLK, 128), F32),
        ),
        in_specs=[HBM] * 4,
        out_specs=(VMEM, VMEM),
        scratch_shapes=[
            pltpu.VMEM((LI * BLK, LQ * BLK), F32),
            pltpu.VMEM((SHARE, COLS), F32),
            pltpu.SMEM((8, 128), jnp.int32),
            pltpu.SMEM((8, 128), jnp.int32),
            pltpu.SMEM((16,), jnp.int32),
            pltpu.SMEM((16,), jnp.int32),
            pltpu.SemaphoreType.DMA((4,)),
        ],
        compiler_params=PARAMS,
        cost_estimate=cost(0, 1 << 20),
    )(*in_hbm(args))


def call_tables(*args):
    return pl.pallas_call(
        tables,
        out_shape=jax.ShapeDtypeStruct((16, 128), jnp.int32),
        in_specs=[HBM] * 2,
        out_specs=VMEM,
        scratch_shapes=[
            pltpu.VMEM((8, 128), jnp.int32),
            pltpu.VMEM((64, 128), jnp.int32),
            pltpu.SemaphoreType.DMA((2,)),
        ],
        compiler_params=PARAMS,
        cost_estimate=cost(0, 1 << 18),
    )(*in_hbm(args))


def call_join(parts):
    return pl.pallas_call(
        join,
        out_shape=jax.ShapeDtypeStruct((len(parts) * LPACK, 128), F32),
        in_specs=[VMEM] * len(parts),
        out_specs=VMEM,
        compiler_params=PARAMS,
        cost_estimate=cost(0, 1 << 18),
    )(*parts)


def call_unpack_left(mine, index, lefts):
    return pl.pallas_call(
        functools.partial(unpack_left, mine),
        out_shape=jax.ShapeDtypeStruct((256, NZ * SHARE), BF16),
        in_specs=[SMEM] + [VMEM] * 4,
        out_specs=VMEM,
        compiler_params=PARAMS,
        cost_estimate=cost(0, 1 << 16),
    )(index, *lefts)


def call_unpack_right(offsets, index, shares):
    n = len(offsets)
    return pl.pallas_call(
        functools.partial(unpack_right, offsets),
        out_shape=(jax.ShapeDtypeStruct((n, SHARE, COLS), BF16),) * 2,
        in_specs=[SMEM] + [VMEM] * n,
        out_specs=(VMEM, VMEM),
        scratch_shapes=[pltpu.VMEM((n, 2 * HELD, 128), F32)],
        compiler_params=PARAMS,
        cost_estimate=cost(0, n << 20),
    )(index, *shares)


def call_multiply(index, left, ready, fresh):
    n = len(fresh)
    operands = [array for _, arrays in ready for array in arrays]
    operands += [piece for _, pieces in fresh for piece in pieces]
    count = n + sum(len(offsets) for offsets, _ in ready)
    kernel = functools.partial(
        multiply,
        [offsets for offsets, _ in ready],
        [(offset, len(pieces)) for offset, pieces in fresh],
    )
    return pl.pallas_call(
        kernel,
        out_shape=jax.ShapeDtypeStruct((128, COLS), F32),
        in_specs=[SMEM] + [VMEM] * (1 + len(operands)),
        out_specs=VMEM,
        scratch_shapes=[
            pltpu.VMEM((n, 2 * HELD, 128), F32),
            pltpu.VMEM((n, SHARE, COLS), BF16),
            pltpu.VMEM((n, SHARE, COLS), BF16),
        ],
        compiler_params=PARAMS,
        cost_estimate=cost(count * 3 * ROWS * SHARE * COLS, 4 * ROWS * COLS),
    )(index, left, *operands)


def call_finish(offset, keep, index, left, pieces, total):
    width = COLS // 2
    return pl.pallas_call(
        functools.partial(finish, offset, keep),
        out_shape=jax.ShapeDtypeStruct((128, width), F32),
        in_specs=[SMEM] + [VMEM] * 4,
        out_specs=VMEM,
        scratch_shapes=[
            pltpu.VMEM((2 * HELD, 128), F32),
            pltpu.VMEM((SHARE, width), BF16),
            pltpu.VMEM((SHARE, width), BF16),
        ],
        compiler_params=PARAMS,
        cost_estimate=cost(3 * 128 * SHARE * COLS, ROWS * COLS),
    )(index, left, *pieces, total)


def assemble(mine, theirs, other, rest, out):
    l = lax.axis_index("layer")
    width = COLS // 2
    for half, part in ((l, other), (1 - l, rest)):
        cols = pl.ds(pl.multiple_of(half * width, width), width)
        out[:, cols] = mine[:, cols] + theirs[:, cols] + part[...]


def call_assemble(*args):
    return pl.pallas_call(
        assemble,
        out_shape=jax.ShapeDtypeStruct((128, COLS), F32),
        in_specs=[VMEM] * 4,
        out_specs=VMEM,
        compiler_params=PARAMS,
        cost_estimate=cost(0, 1 << 21),
    )(*args)


def z_perm(d):
    return [(z * 2 + y, ((z + d) % NZ) * 2 + y) for z in range(NZ) for y in range(2)]


def x_perm(d):
    return [(((x + d) % 4) * 2 + y, x * 2 + y) for x in range(4) for y in range(2)]


def local(left_tensor, right_tensor, left_occupied, right_occupied):
    left0, right0 = call_pack(left_tensor, right_tensor, left_occupied, right_occupied)
    index = call_tables(left_occupied, right_occupied)

    pair = [(r, r ^ 1) for r in range(16)]
    near = lambda dy, dh: [(r * 8 + c, (r ^ dy) * 8 + (c ^ dh)) for r in range(16) for c in range(8)]
    z_send = lambda v, d: lax.ppermute(v, "row", z_perm(d))
    up1, down1 = z_send(right0, 1), z_send(right0, -1)
    nears = [lax.ppermute(left0, ("row", "col"), near(dy, dh)) for dy, dh in ((1, 0), (0, 1), (1, 1))]
    rights0 = call_unpack_right((0,), index, (right0,))
    up1, down1, rights0, *nears = lax.optimization_barrier((up1, down1, rights0, *nears))
    left2 = call_join([left0] + nears)
    up2, down2 = z_send(up1, 1), z_send(down1, -1)
    x_send = lambda v, d: lax.ppermute(v, "col", x_perm(d))
    lefts = [left2] + [x_send(left2, d) for d in (1, 2, 3)]
    up3, down3 = z_send(up2, 1), z_send(down2, -1)
    near_z = (-1, 1, -2, 2)
    rights = call_unpack_right(near_z, index, (up1, down1, up2, down2))
    ready = [((0,), rights0), (near_z, rights)]
    third = [(-3, (up3,)), (3, (down3,))]
    half = SLABS * BLK // 2
    far = z_send(up3[:half], 1), z_send(down3[half:], -1)

    left = call_unpack_left(False, index, lefts)
    swap = [(0, 1), (1, 0)]
    total = call_multiply(index, left, ready, third)
    give = call_finish(4, False, index, left, far, total)
    recv = lax.ppermute(give, "layer", swap)
    keep = call_finish(4, True, index, left, far, total)
    send = keep + recv
    other = lax.ppermute(send, "row", pair)
    index, send = lax.optimization_barrier((index, send))
    own = call_unpack_left(True, index, lefts)
    mine = call_multiply(index, own, ready, third + [(4, far)])
    theirs = lax.ppermute(mine, "layer", swap)
    rest = lax.ppermute(other, "layer", swap)
    return call_assemble(mine, theirs, other, rest)


def solution(mesh):
    placed = (P("row", ("layer", "col")), P(("layer", "row"), "col"), P(), P())
    return jax.shard_map(
        local, mesh=mesh, in_specs=placed, out_specs=P("row", "col"), check_vma=False
    )
```

```python
import functools

import jax
import jax.numpy as jnp
from jax import lax
from jax.experimental import pallas as pl
from jax.experimental.pallas import tpu as pltpu
from jax.sharding import PartitionSpec as P


BLK = 64
KB = 4
JB = 16
LI, LQ = 2, 8
RCAP, LCAP = 12, 3
NZ, NC = 8, 8
SHARE = KB * BLK
COLS = JB * BLK
ROWS = 2 * LI * BLK
SLABS = RCAP // 2
LPACK = 96
F32, BF16 = jnp.float32, jnp.bfloat16
VMEM = pl.BlockSpec(memory_space=pltpu.VMEM)
SMEM = pl.BlockSpec(memory_space=pltpu.SMEM)
HBM = pl.BlockSpec(memory_space=pltpu.HBM)
PARAMS = pltpu.CompilerParams(vmem_limit_bytes=32 * 1024 * 1024)
EMPTY = RCAP
HELD = (SLABS + 1) * BLK


def place():
    r = lax.axis_index("row")
    return lax.axis_index("layer"), r // 2, r % 2, lax.axis_index("col")


def low_half(shape):
    return lax.broadcasted_iota(jnp.int32, shape, 1) < BLK


def cost(flops, moved):
    return pl.CostEstimate(flops=flops, bytes_accessed=moved, transcendentals=0)


def block_at(ref, e, per_row, odd):
    k, j = e // per_row, e % per_row
    v = ref[
        pl.ds(pl.multiple_of(k * BLK, BLK), BLK),
        pl.ds(pl.multiple_of((j // 2) * 128, 128), 128),
    ]
    return jnp.where(j % 2 == odd, v, pltpu.roll(v, BLK, 1))


def ranks(flags, per_row, rows, none):
    n = flags.shape[0]
    f = flags.astype(F32)
    a, b = grid((128, 128))
    same = a // per_row == b // per_row
    in_row = pick(f, same & (a < b))
    row_sum = pick(f, same)
    a, b = grid((n, n))
    before = pick((a // rows == b // rows) & (b < a), row_sum)
    return jnp.where(f > 0, in_row + before, none)


def grid(shape):
    return [lax.broadcasted_iota(jnp.int32, shape, d) for d in (0, 1)]


def pick(a, b):
    return jnp.dot(
        a.astype(F32).astype(BF16), b.astype(F32).astype(BF16), preferred_element_type=F32
    )


def pack(
    left_hbm, right_hbm, left_occupied, right_occupied, left_out, right_out,
    left, right, lflags, rflags, lindex, rindex, sems,
):
    l, z, y, c = place()
    ltop = pl.multiple_of((z // 2) * 8, 8)
    rtop = pl.multiple_of(l * 64 + z * 8, 8)
    copies = [
        pltpu.make_async_copy(right_occupied.at[pl.ds(rtop, 8)], rflags, sems.at[0]),
        pltpu.make_async_copy(left_occupied.at[pl.ds(ltop, 8)], lflags, sems.at[1]),
        pltpu.make_async_copy(right_hbm, right, sems.at[2]),
        pltpu.make_async_copy(left_hbm, left, sems.at[3]),
    ]
    for copy in copies:
        copy.start()
    copies[0].wait()
    rcount = jnp.int32(0)
    for k in range(KB):
        for j in range(JB):
            rindex[rcount] = k * JB + j
            rcount += rflags[y * KB + k, c * JB + j]
    copies[1].wait()
    lcount = jnp.int32(0)
    for i in range(LI):
        for q in range(LQ):
            lindex[lcount] = i * LQ + q
            lcount += lflags[(z % 2) * 4 + y * LI + i, l * 64 + c * LQ + q]
    low = low_half((BLK, 128))
    copies[2].wait()
    for p in range(SLABS):
        ea = jnp.where(2 * p < rcount, rindex[2 * p], 0)
        eb = jnp.where(2 * p + 1 < rcount, rindex[2 * p + 1], 0)
        right_out[p * BLK : (p + 1) * BLK, :] = jnp.where(
            low, block_at(right, ea, JB, 0), block_at(right, eb, JB, 1)
        )
    copies[3].wait()
    e = [jnp.where(s < lcount, lindex[s], 0) for s in range(LCAP)]
    left_out[:BLK, :] = jnp.where(low, block_at(left, e[0], LQ, 0), block_at(left, e[1], LQ, 1))
    a = block_at(left, e[2], LQ, 0)
    b = block_at(left, e[2], LQ, 1)
    left_out[BLK:, :] = jnp.where(low_half((BLK // 2, 128)), a[: BLK // 2], b[BLK // 2 :])


def tables(left_occupied, right_occupied, slots, lall, rall, sems):
    l, z, y, c = place()
    ltop = pl.multiple_of((z // 2) * 8, 8)
    ptop = pl.multiple_of(l * 64, 64)
    copies = [
        pltpu.make_async_copy(right_occupied.at[pl.ds(ptop, 64)], rall, sems.at[0]),
        pltpu.make_async_copy(left_occupied.at[pl.ds(ltop, 8)], lall, sems.at[1]),
    ]
    for copy in copies:
        copy.start()
    for copy in copies:
        copy.wait()
    rank = ranks(rall[...], JB, KB, float(EMPTY))
    a, b = grid((8, 64))
    g, h = grid((128, 128))
    total = jnp.zeros((8, 128), F32)
    for k in range(KB):
        row = pick(b == a * 8 + y * KB + k, rank)
        total += pick(row, (h // JB == k) & (g == c * JB + h % JB))
    slots[:8, :] = total.astype(jnp.int32)
    rank = ranks(lall[...], LQ, LI, -1.0)
    a, b = grid((8, 8))
    row = pick(b == (z % 2) * 4 + a, rank)
    row = pick(row, (h < 32) & (g == l * 64 + (h // KB) * LQ + y * KB + h % KB))
    slots[8:, :] = row.astype(jnp.int32)


def join(*refs):
    *parts, out = refs
    for t, part in enumerate(parts):
        out[t * LPACK : (t + 1) * LPACK, :] = part[...]


def split(v):
    h = v.astype(BF16)
    return h, (v - h.astype(F32)).astype(BF16)


def unpack_left(mine, index, a0, a1, a2, a3, out):
    l, z, y, c = place()
    x = c // 2
    low = low_half((BLK, 128))
    low2 = low_half((BLK // 2, 128))
    for d, ref in enumerate((a0, a1, a2, a3)):
        for part in (0, 2) if mine else (1, 3):
            yh = (c % 2) ^ (part // 2)
            yl = y ^ (part % 2)
            column = ((x + d) % 4) * 2 + yh
            base = part * LPACK
            v = ref[base : base + BLK, :]
            w = ref[base + BLK : base + LPACK, :]
            vr, wr = pltpu.roll(v, BLK, 1), pltpu.roll(w, BLK, 1)
            s0 = jnp.where(low, v, vr)
            s1 = jnp.where(low, vr, v)
            s2 = jnp.concatenate([jnp.where(low2, w, wr), jnp.where(low2, wr, w)], axis=0)
            for i in range(LI):
                for p in range(KB // 2):
                    at = column * KB + 2 * p
                    slot = jnp.where(low, index[8 + yl * LI + i, at], index[8 + yl * LI + i, at + 1])
                    t = jnp.where(slot == 0, s0, jnp.where(slot == 1, s1, jnp.where(slot == 2, s2, 0.0)))
                    lanes = pl.ds(pl.multiple_of(column * SHARE + p * 128, 128), 128)
                    h, g = split(t)
                    out[i * BLK : (i + 1) * BLK, lanes] = h
                    out[128 + i * BLK : 128 + (i + 1) * BLK, lanes] = g


def spread(index, source, pieces, two, hi, lo, first=0):
    low = low_half((BLK, 128))
    top = 0
    for piece in pieces:
        v = piece[...]
        n = v.shape[0]
        two[top : top + n, :] = v
        two[HELD + top : HELD + top + n, :] = pltpu.roll(v, BLK, 1)
        top += n
    two[SLABS * BLK : HELD, :] = jnp.zeros((BLK, 128), F32)
    two[HELD + SLABS * BLK :, :] = jnp.zeros((BLK, 128), F32)
    for k in range(KB):
        for p in range(hi.shape[1] // 128):
            s0 = index[source, k * JB + 2 * (first + p)]
            s1 = index[source, k * JB + 2 * (first + p) + 1]
            r0 = (s0 & 1) * HELD + lax.shift_right_logical(s0, 1) * BLK
            r1 = (1 - (s1 & 1)) * HELD + lax.shift_right_logical(s1, 1) * BLK
            v0 = two[pl.ds(pl.multiple_of(r0, BLK), BLK), :]
            v1 = two[pl.ds(pl.multiple_of(r1, BLK), BLK), :]
            h, g = split(jnp.where(low, v0, v1))
            hi[k * BLK : (k + 1) * BLK, p * 128 : (p + 1) * 128] = h
            lo[k * BLK : (k + 1) * BLK, p * 128 : (p + 1) * 128] = g


def unpack_right(offsets, index, *refs):
    n = len(offsets)
    shares, (hi, lo, two) = refs[:n], refs[n:]
    l, z, y, c = place()
    for t, offset in enumerate(offsets):
        spread(index, (z + offset) % NZ, shares[t : t + 1], two.at[t], hi.at[t], lo.at[t])


def product(left, ks, hi, lo):
    dot = functools.partial(jnp.dot, preferred_element_type=F32)
    big = dot(left[:, ks], hi)
    return (big[128:] + dot(left[:128, ks], lo)) + big[:128]


def finish(offset, keep, index, left, share0, share1, total, out, two, hi, lo):
    l, z, y, c = place()
    source = (z + offset) % NZ
    half = l if keep else 1 - l
    spread(index, source, (share0, share1), two, hi, lo, half * (JB // 4))
    ks = pl.ds(pl.multiple_of(source * SHARE, SHARE), SHARE)
    width = COLS // 2
    for n0 in range(0, width, 256):
        cols = pl.ds(pl.multiple_of(half * width + n0, 256), 256)
        out[:, n0 : n0 + 256] = total[:, cols] + product(
            left, ks, hi[:, n0 : n0 + 256], lo[:, n0 : n0 + 256]
        )


def multiply(ready, fresh, index, left, *refs):
    refs = list(refs)
    take = lambda n: [refs.pop(0) for _ in range(n)]
    l, z, y, c = place()
    parts = []
    for group in ready:
        hi, lo = take(2)
        parts += [(offset, hi.at[t], lo.at[t]) for t, offset in enumerate(group)]
    shares = [take(n) for _, n in fresh]
    out, two, hi, lo = refs
    for t, (offset, _) in enumerate(fresh):
        spread(index, (z + offset) % NZ, shares[t], two.at[t], hi.at[t], lo.at[t])
        parts.append((offset, hi.at[t], lo.at[t]))
    for n0 in range(0, COLS, 256):
        cols = slice(n0, n0 + 256)
        done = None
        for offset, h, g in parts:
            ks = pl.ds(pl.multiple_of(((z + offset) % NZ) * SHARE, SHARE), SHARE)
            one = product(left, ks, h[:, cols], g[:, cols])
            done = one if done is None else done + one
        out[:, cols] = done


def in_hbm(arrays):
    return [pltpu.with_memory_space_constraint(a, pltpu.HBM) for a in arrays]


def call_pack(*args):
    return pl.pallas_call(
        pack,
        out_shape=(
            jax.ShapeDtypeStruct((LPACK, 128), F32),
            jax.ShapeDtypeStruct((SLABS * BLK, 128), F32),
        ),
        in_specs=[HBM] * 4,
        out_specs=(VMEM, VMEM),
        scratch_shapes=[
            pltpu.VMEM((LI * BLK, LQ * BLK), F32),
            pltpu.VMEM((SHARE, COLS), F32),
            pltpu.SMEM((8, 128), jnp.int32),
            pltpu.SMEM((8, 128), jnp.int32),
            pltpu.SMEM((16,), jnp.int32),
            pltpu.SMEM((16,), jnp.int32),
            pltpu.SemaphoreType.DMA((4,)),
        ],
        compiler_params=PARAMS,
        cost_estimate=cost(0, 1 << 20),
    )(*in_hbm(args))


def call_tables(*args):
    return pl.pallas_call(
        tables,
        out_shape=jax.ShapeDtypeStruct((16, 128), jnp.int32),
        in_specs=[HBM] * 2,
        out_specs=VMEM,
        scratch_shapes=[
            pltpu.VMEM((8, 128), jnp.int32),
            pltpu.VMEM((64, 128), jnp.int32),
            pltpu.SemaphoreType.DMA((2,)),
        ],
        compiler_params=PARAMS,
        cost_estimate=cost(0, 1 << 18),
    )(*in_hbm(args))


def call_join(parts):
    return pl.pallas_call(
        join,
        out_shape=jax.ShapeDtypeStruct((len(parts) * LPACK, 128), F32),
        in_specs=[VMEM] * len(parts),
        out_specs=VMEM,
        compiler_params=PARAMS,
        cost_estimate=cost(0, 1 << 18),
    )(*parts)


def call_unpack_left(mine, index, lefts):
    return pl.pallas_call(
        functools.partial(unpack_left, mine),
        out_shape=jax.ShapeDtypeStruct((256, NZ * SHARE), BF16),
        in_specs=[SMEM] + [VMEM] * 4,
        out_specs=VMEM,
        compiler_params=PARAMS,
        cost_estimate=cost(0, 1 << 16),
    )(index, *lefts)


def call_unpack_right(offsets, index, shares):
    n = len(offsets)
    return pl.pallas_call(
        functools.partial(unpack_right, offsets),
        out_shape=(jax.ShapeDtypeStruct((n, SHARE, COLS), BF16),) * 2,
        in_specs=[SMEM] + [VMEM] * n,
        out_specs=(VMEM, VMEM),
        scratch_shapes=[pltpu.VMEM((n, 2 * HELD, 128), F32)],
        compiler_params=PARAMS,
        cost_estimate=cost(0, n << 20),
    )(index, *shares)


def call_multiply(index, left, ready, fresh):
    n = len(fresh)
    operands = [array for _, arrays in ready for array in arrays]
    operands += [piece for _, pieces in fresh for piece in pieces]
    count = n + sum(len(offsets) for offsets, _ in ready)
    kernel = functools.partial(
        multiply,
        [offsets for offsets, _ in ready],
        [(offset, len(pieces)) for offset, pieces in fresh],
    )
    return pl.pallas_call(
        kernel,
        out_shape=jax.ShapeDtypeStruct((128, COLS), F32),
        in_specs=[SMEM] + [VMEM] * (1 + len(operands)),
        out_specs=VMEM,
        scratch_shapes=[
            pltpu.VMEM((n, 2 * HELD, 128), F32),
            pltpu.VMEM((n, SHARE, COLS), BF16),
            pltpu.VMEM((n, SHARE, COLS), BF16),
        ],
        compiler_params=PARAMS,
        cost_estimate=cost(count * 3 * ROWS * SHARE * COLS, 4 * ROWS * COLS),
    )(index, left, *operands)


def call_finish(offset, keep, index, left, pieces, total):
    width = COLS // 2
    return pl.pallas_call(
        functools.partial(finish, offset, keep),
        out_shape=jax.ShapeDtypeStruct((128, width), F32),
        in_specs=[SMEM] + [VMEM] * 4,
        out_specs=VMEM,
        scratch_shapes=[
            pltpu.VMEM((2 * HELD, 128), F32),
            pltpu.VMEM((SHARE, width), BF16),
            pltpu.VMEM((SHARE, width), BF16),
        ],
        compiler_params=PARAMS,
        cost_estimate=cost(3 * 128 * SHARE * COLS, ROWS * COLS),
    )(index, left, *pieces, total)


def assemble(mine, theirs, other, rest, out):
    l = lax.axis_index("layer")
    width = COLS // 2
    for half, part in ((l, other), (1 - l, rest)):
        cols = pl.ds(pl.multiple_of(half * width, width), width)
        out[:, cols] = mine[:, cols] + theirs[:, cols] + part[...]


def call_assemble(*args):
    return pl.pallas_call(
        assemble,
        out_shape=jax.ShapeDtypeStruct((128, COLS), F32),
        in_specs=[VMEM] * 4,
        out_specs=VMEM,
        compiler_params=PARAMS,
        cost_estimate=cost(0, 1 << 21),
    )(*args)


def z_perm(d):
    return [(z * 2 + y, ((z + d) % NZ) * 2 + y) for z in range(NZ) for y in range(2)]


def x_perm(d):
    return [(((x + d) % 4) * 2 + y, x * 2 + y) for x in range(4) for y in range(2)]


def local(left_tensor, right_tensor, left_occupied, right_occupied):
    left0, right0 = call_pack(left_tensor, right_tensor, left_occupied, right_occupied)
    index = call_tables(left_occupied, right_occupied)

    pair = [(r, r ^ 1) for r in range(16)]
    near = lambda dy, dh: [(r * 8 + c, (r ^ dy) * 8 + (c ^ dh)) for r in range(16) for c in range(8)]
    z_send = lambda v, d: lax.ppermute(v, "row", z_perm(d))
    up1, down1 = z_send(right0, 1), z_send(right0, -1)
    send_near = lambda dy, dh: lax.ppermute(left0, ("row", "col"), near(dy, dh))
    both, over_h, over_y = send_near(1, 1), send_near(0, 1), send_near(1, 0)
    nears = [over_y, over_h, both]
    up1, down1, index, *nears = lax.optimization_barrier((up1, down1, index, *nears))
    left2 = call_join([left0] + nears)
    up2, down2 = z_send(up1, 1), z_send(down1, -1)
    x_send = lambda v, d: lax.ppermute(v, "col", x_perm(d))
    lefts = [left2] + [x_send(left2, d) for d in (1, 2, 3)]
    up3, down3 = z_send(up2, 1), z_send(down2, -1)
    near_z = (0, -1, 1, -2, 2)
    rights = call_unpack_right(near_z, index, (right0, up1, down1, up2, down2))
    ready = [(near_z, rights)]
    third = [(-3, (up3,)), (3, (down3,))]
    half = SLABS * BLK // 2
    far = z_send(up3[:half], 1), z_send(down3[half:], -1)

    left = call_unpack_left(False, index, lefts)
    swap = [(0, 1), (1, 0)]
    total = call_multiply(index, left, ready, third)
    give = call_finish(4, False, index, left, far, total)
    recv = lax.ppermute(give, "layer", swap)
    keep = call_finish(4, True, index, left, far, total)
    send = keep + recv
    other = lax.ppermute(send, "row", pair)
    index, send = lax.optimization_barrier((index, send))
    own = call_unpack_left(True, index, lefts)
    mine = call_multiply(index, own, ready, third + [(4, far)])
    theirs = lax.ppermute(mine, "layer", swap)
    rest = lax.ppermute(other, "layer", swap)
    return call_assemble(mine, theirs, other, rest)


def solution(mesh):
    placed = (P("row", ("layer", "col")), P(("layer", "row"), "col"), P(), P())
    return jax.shard_map(
        local, mesh=mesh, in_specs=placed, out_specs=P("row", "col"), check_vma=False
    )
```

```python
import functools

import jax
import jax.numpy as jnp
from jax import lax
from jax.experimental import pallas as pl
from jax.experimental.pallas import tpu as pltpu
from jax.sharding import PartitionSpec as P


BLK = 64
KB = 4
JB = 16
LI, LQ = 2, 8
RCAP, LCAP = 12, 3
NZ, NC = 8, 8
SHARE = KB * BLK
COLS = JB * BLK
ROWS = 2 * LI * BLK
SLABS = RCAP // 2
LPACK = 96
F32, BF16 = jnp.float32, jnp.bfloat16
VMEM = pl.BlockSpec(memory_space=pltpu.VMEM)
SMEM = pl.BlockSpec(memory_space=pltpu.SMEM)
HBM = pl.BlockSpec(memory_space=pltpu.HBM)
PARAMS = pltpu.CompilerParams(vmem_limit_bytes=32 * 1024 * 1024)
EMPTY = RCAP
HELD = (SLABS + 1) * BLK


def place():
    r = lax.axis_index("row")
    return lax.axis_index("layer"), r // 2, r % 2, lax.axis_index("col")


def low_half(shape):
    return lax.broadcasted_iota(jnp.int32, shape, 1) < BLK


def cost(flops, moved):
    return pl.CostEstimate(flops=flops, bytes_accessed=moved, transcendentals=0)


def block_at(ref, e, per_row, odd):
    k, j = e // per_row, e % per_row
    v = ref[
        pl.ds(pl.multiple_of(k * BLK, BLK), BLK),
        pl.ds(pl.multiple_of((j // 2) * 128, 128), 128),
    ]
    return jnp.where(j % 2 == odd, v, pltpu.roll(v, BLK, 1))


def ranks(flags, per_row, rows, none):
    n = flags.shape[0]
    f = flags.astype(F32)
    a, b = grid((128, 128))
    same = a // per_row == b // per_row
    in_row = pick(f, same & (a < b))
    row_sum = pick(f, same)
    a, b = grid((n, n))
    before = pick((a // rows == b // rows) & (b < a), row_sum)
    return jnp.where(f > 0, in_row + before, none)


def grid(shape):
    return [lax.broadcasted_iota(jnp.int32, shape, d) for d in (0, 1)]


def pick(a, b):
    return jnp.dot(
        a.astype(F32).astype(BF16), b.astype(F32).astype(BF16), preferred_element_type=F32
    )


def pack(
    left_hbm, right_hbm, left_occupied, right_occupied, left_out, right_out,
    left, right, lflags, rflags, lindex, rindex, sems,
):
    l, z, y, c = place()
    ltop = pl.multiple_of((z // 2) * 8, 8)
    rtop = pl.multiple_of(l * 64 + z * 8, 8)
    copies = [
        pltpu.make_async_copy(right_occupied.at[pl.ds(rtop, 8)], rflags, sems.at[0]),
        pltpu.make_async_copy(left_occupied.at[pl.ds(ltop, 8)], lflags, sems.at[1]),
        pltpu.make_async_copy(right_hbm, right, sems.at[2]),
        pltpu.make_async_copy(left_hbm, left, sems.at[3]),
    ]
    for copy in copies:
        copy.start()
    copies[0].wait()
    rcount = jnp.int32(0)
    for k in range(KB):
        for j in range(JB):
            rindex[rcount] = k * JB + j
            rcount += rflags[y * KB + k, c * JB + j]
    copies[1].wait()
    lcount = jnp.int32(0)
    for i in range(LI):
        for q in range(LQ):
            lindex[lcount] = i * LQ + q
            lcount += lflags[(z % 2) * 4 + y * LI + i, l * 64 + c * LQ + q]
    low = low_half((BLK, 128))
    copies[2].wait()
    for p in range(SLABS):
        ea = jnp.where(2 * p < rcount, rindex[2 * p], 0)
        eb = jnp.where(2 * p + 1 < rcount, rindex[2 * p + 1], 0)
        right_out[p * BLK : (p + 1) * BLK, :] = jnp.where(
            low, block_at(right, ea, JB, 0), block_at(right, eb, JB, 1)
        )
    copies[3].wait()
    e = [jnp.where(s < lcount, lindex[s], 0) for s in range(LCAP)]
    left_out[:BLK, :] = jnp.where(low, block_at(left, e[0], LQ, 0), block_at(left, e[1], LQ, 1))
    a = block_at(left, e[2], LQ, 0)
    b = block_at(left, e[2], LQ, 1)
    left_out[BLK:, :] = jnp.where(low_half((BLK // 2, 128)), a[: BLK // 2], b[BLK // 2 :])


def tables(left_occupied, right_occupied, slots, lall, rall, sems):
    l, z, y, c = place()
    ltop = pl.multiple_of((z // 2) * 8, 8)
    ptop = pl.multiple_of(l * 64, 64)
    copies = [
        pltpu.make_async_copy(right_occupied.at[pl.ds(ptop, 64)], rall, sems.at[0]),
        pltpu.make_async_copy(left_occupied.at[pl.ds(ltop, 8)], lall, sems.at[1]),
    ]
    for copy in copies:
        copy.start()
    for copy in copies:
        copy.wait()
    rank = ranks(rall[...], JB, KB, float(EMPTY))
    a, b = grid((8, 64))
    g, h = grid((128, 128))
    total = jnp.zeros((8, 128), F32)
    for k in range(KB):
        row = pick(b == a * 8 + y * KB + k, rank)
        total += pick(row, (h // JB == k) & (g == c * JB + h % JB))
    slots[:8, :] = total.astype(jnp.int32)
    rank = ranks(lall[...], LQ, LI, -1.0)
    a, b = grid((8, 8))
    row = pick(b == (z % 2) * 4 + a, rank)
    row = pick(row, (h < 32) & (g == l * 64 + (h // KB) * LQ + y * KB + h % KB))
    slots[8:, :] = row.astype(jnp.int32)


def join(*refs):
    *parts, out = refs
    for t, part in enumerate(parts):
        out[t * LPACK : (t + 1) * LPACK, :] = part[...]


def split(v):
    h = v.astype(BF16)
    return h, (v - h.astype(F32)).astype(BF16)


def unpack_left(mine, index, a0, a1, a2, a3, out):
    l, z, y, c = place()
    x = c // 2
    low = low_half((BLK, 128))
    low2 = low_half((BLK // 2, 128))
    for d, ref in enumerate((a0, a1, a2, a3)):
        for part in (0, 2) if mine else (1, 3):
            yh = (c % 2) ^ (part // 2)
            yl = y ^ (part % 2)
            column = ((x + d) % 4) * 2 + yh
            base = part * LPACK
            v = ref[base : base + BLK, :]
            w = ref[base + BLK : base + LPACK, :]
            vr, wr = pltpu.roll(v, BLK, 1), pltpu.roll(w, BLK, 1)
            s0 = jnp.where(low, v, vr)
            s1 = jnp.where(low, vr, v)
            s2 = jnp.concatenate([jnp.where(low2, w, wr), jnp.where(low2, wr, w)], axis=0)
            for i in range(LI):
                for p in range(KB // 2):
                    at = column * KB + 2 * p
                    slot = jnp.where(low, index[8 + yl * LI + i, at], index[8 + yl * LI + i, at + 1])
                    t = jnp.where(slot == 0, s0, jnp.where(slot == 1, s1, jnp.where(slot == 2, s2, 0.0)))
                    lanes = pl.ds(pl.multiple_of(column * SHARE + p * 128, 128), 128)
                    h, g = split(t)
                    out[i * BLK : (i + 1) * BLK, lanes] = h
                    out[128 + i * BLK : 128 + (i + 1) * BLK, lanes] = g


def spread(index, source, pieces, two, hi, lo, first=0):
    low = low_half((BLK, 128))
    top = 0
    for piece in pieces:
        v = piece[...]
        n = v.shape[0]
        two[top : top + n, :] = v
        two[HELD + top : HELD + top + n, :] = pltpu.roll(v, BLK, 1)
        top += n
    two[SLABS * BLK : HELD, :] = jnp.zeros((BLK, 128), F32)
    two[HELD + SLABS * BLK :, :] = jnp.zeros((BLK, 128), F32)
    for k in range(KB):
        for p in range(hi.shape[1] // 128):
            s0 = index[source, k * JB + 2 * (first + p)]
            s1 = index[source, k * JB + 2 * (first + p) + 1]
            r0 = (s0 & 1) * HELD + lax.shift_right_logical(s0, 1) * BLK
            r1 = (1 - (s1 & 1)) * HELD + lax.shift_right_logical(s1, 1) * BLK
            v0 = two[pl.ds(pl.multiple_of(r0, BLK), BLK), :]
            v1 = two[pl.ds(pl.multiple_of(r1, BLK), BLK), :]
            h, g = split(jnp.where(low, v0, v1))
            hi[k * BLK : (k + 1) * BLK, p * 128 : (p + 1) * 128] = h
            lo[k * BLK : (k + 1) * BLK, p * 128 : (p + 1) * 128] = g


def unpack_right(offsets, index, *refs):
    n = len(offsets)
    shares, (hi, lo, two) = refs[:n], refs[n:]
    l, z, y, c = place()
    for t, offset in enumerate(offsets):
        spread(index, (z + offset) % NZ, shares[t : t + 1], two.at[t], hi.at[t], lo.at[t])


def product(left, ks, hi, lo):
    dot = functools.partial(jnp.dot, preferred_element_type=F32)
    big = dot(left[:, ks], hi)
    return (big[128:] + dot(left[:128, ks], lo)) + big[:128]


def finish(offset, keep, index, left, share0, share1, total, out, two, hi, lo):
    l, z, y, c = place()
    source = (z + offset) % NZ
    half = l if keep else 1 - l
    spread(index, source, (share0, share1), two, hi, lo, half * (JB // 4))
    ks = pl.ds(pl.multiple_of(source * SHARE, SHARE), SHARE)
    width = COLS // 2
    for n0 in range(0, width, 256):
        cols = pl.ds(pl.multiple_of(half * width + n0, 256), 256)
        out[:, n0 : n0 + 256] = total[:, cols] + product(
            left, ks, hi[:, n0 : n0 + 256], lo[:, n0 : n0 + 256]
        )


def multiply(ready, fresh, index, left, *refs):
    refs = list(refs)
    take = lambda n: [refs.pop(0) for _ in range(n)]
    l, z, y, c = place()
    parts = []
    for group in ready:
        hi, lo = take(2)
        parts += [(offset, hi.at[t], lo.at[t]) for t, offset in enumerate(group)]
    shares = [take(n) for _, n in fresh]
    out, two, hi, lo = refs
    for t, (offset, _) in enumerate(fresh):
        spread(index, (z + offset) % NZ, shares[t], two.at[t], hi.at[t], lo.at[t])
        parts.append((offset, hi.at[t], lo.at[t]))
    for n0 in range(0, COLS, 256):
        cols = slice(n0, n0 + 256)
        done = None
        for offset, h, g in parts:
            ks = pl.ds(pl.multiple_of(((z + offset) % NZ) * SHARE, SHARE), SHARE)
            one = product(left, ks, h[:, cols], g[:, cols])
            done = one if done is None else done + one
        out[:, cols] = done


def in_hbm(arrays):
    return [pltpu.with_memory_space_constraint(a, pltpu.HBM) for a in arrays]


def call_pack(*args):
    return pl.pallas_call(
        pack,
        out_shape=(
            jax.ShapeDtypeStruct((LPACK, 128), F32),
            jax.ShapeDtypeStruct((SLABS * BLK, 128), F32),
        ),
        in_specs=[HBM] * 4,
        out_specs=(VMEM, VMEM),
        scratch_shapes=[
            pltpu.VMEM((LI * BLK, LQ * BLK), F32),
            pltpu.VMEM((SHARE, COLS), F32),
            pltpu.SMEM((8, 128), jnp.int32),
            pltpu.SMEM((8, 128), jnp.int32),
            pltpu.SMEM((16,), jnp.int32),
            pltpu.SMEM((16,), jnp.int32),
            pltpu.SemaphoreType.DMA((4,)),
        ],
        compiler_params=PARAMS,
        cost_estimate=cost(0, 1 << 20),
    )(*in_hbm(args))


def call_tables(*args):
    return pl.pallas_call(
        tables,
        out_shape=jax.ShapeDtypeStruct((16, 128), jnp.int32),
        in_specs=[HBM] * 2,
        out_specs=VMEM,
        scratch_shapes=[
            pltpu.VMEM((8, 128), jnp.int32),
            pltpu.VMEM((64, 128), jnp.int32),
            pltpu.SemaphoreType.DMA((2,)),
        ],
        compiler_params=PARAMS,
        cost_estimate=cost(0, 1 << 18),
    )(*in_hbm(args))


def call_join(parts):
    return pl.pallas_call(
        join,
        out_shape=jax.ShapeDtypeStruct((len(parts) * LPACK, 128), F32),
        in_specs=[VMEM] * len(parts),
        out_specs=VMEM,
        compiler_params=PARAMS,
        cost_estimate=cost(0, 1 << 18),
    )(*parts)


def call_unpack_left(mine, index, lefts):
    return pl.pallas_call(
        functools.partial(unpack_left, mine),
        out_shape=jax.ShapeDtypeStruct((256, NZ * SHARE), BF16),
        in_specs=[SMEM] + [VMEM] * 4,
        out_specs=VMEM,
        compiler_params=PARAMS,
        cost_estimate=cost(0, 1 << 16),
    )(index, *lefts)


def call_unpack_right(offsets, index, shares):
    n = len(offsets)
    return pl.pallas_call(
        functools.partial(unpack_right, offsets),
        out_shape=(jax.ShapeDtypeStruct((n, SHARE, COLS), BF16),) * 2,
        in_specs=[SMEM] + [VMEM] * n,
        out_specs=(VMEM, VMEM),
        scratch_shapes=[pltpu.VMEM((n, 2 * HELD, 128), F32)],
        compiler_params=PARAMS,
        cost_estimate=cost(0, n << 20),
    )(index, *shares)


def call_multiply(index, left, ready, fresh):
    n = len(fresh)
    operands = [array for _, arrays in ready for array in arrays]
    operands += [piece for _, pieces in fresh for piece in pieces]
    count = n + sum(len(offsets) for offsets, _ in ready)
    kernel = functools.partial(
        multiply,
        [offsets for offsets, _ in ready],
        [(offset, len(pieces)) for offset, pieces in fresh],
    )
    return pl.pallas_call(
        kernel,
        out_shape=jax.ShapeDtypeStruct((128, COLS), F32),
        in_specs=[SMEM] + [VMEM] * (1 + len(operands)),
        out_specs=VMEM,
        scratch_shapes=[
            pltpu.VMEM((n, 2 * HELD, 128), F32),
            pltpu.VMEM((n, SHARE, COLS), BF16),
            pltpu.VMEM((n, SHARE, COLS), BF16),
        ],
        compiler_params=PARAMS,
        cost_estimate=cost(count * 3 * ROWS * SHARE * COLS, 4 * ROWS * COLS),
    )(index, left, *operands)


def call_finish(offset, keep, index, left, pieces, total):
    width = COLS // 2
    return pl.pallas_call(
        functools.partial(finish, offset, keep),
        out_shape=jax.ShapeDtypeStruct((128, width), F32),
        in_specs=[SMEM] + [VMEM] * 4,
        out_specs=VMEM,
        scratch_shapes=[
            pltpu.VMEM((2 * HELD, 128), F32),
            pltpu.VMEM((SHARE, width), BF16),
            pltpu.VMEM((SHARE, width), BF16),
        ],
        compiler_params=PARAMS,
        cost_estimate=cost(3 * 128 * SHARE * COLS, ROWS * COLS),
    )(index, left, *pieces, total)


def assemble(mine, theirs, other, rest, out):
    l = lax.axis_index("layer")
    width = COLS // 2
    for half, part in ((l, other), (1 - l, rest)):
        cols = pl.ds(pl.multiple_of(half * width, width), width)
        out[:, cols] = mine[:, cols] + theirs[:, cols] + part[...]


def call_assemble(*args):
    return pl.pallas_call(
        assemble,
        out_shape=jax.ShapeDtypeStruct((128, COLS), F32),
        in_specs=[VMEM] * 4,
        out_specs=VMEM,
        compiler_params=PARAMS,
        cost_estimate=cost(0, 1 << 21),
    )(*args)


def z_perm(d):
    return [(z * 2 + y, ((z + d) % NZ) * 2 + y) for z in range(NZ) for y in range(2)]


def x_perm(d):
    return [(((x + d) % 4) * 2 + y, x * 2 + y) for x in range(4) for y in range(2)]


def local(left_tensor, right_tensor, left_occupied, right_occupied):
    left0, right0 = call_pack(left_tensor, right_tensor, left_occupied, right_occupied)
    index = call_tables(left_occupied, right_occupied)

    pair = [(r, r ^ 1) for r in range(16)]
    near = lambda dy, dh: [(r * 8 + c, (r ^ dy) * 8 + (c ^ dh)) for r in range(16) for c in range(8)]
    z_send = lambda v, d: lax.ppermute(v, "row", z_perm(d))
    up1, down1 = z_send(right0, 1), z_send(right0, -1)
    send_near = lambda dy, dh: lax.ppermute(left0, ("row", "col"), near(dy, dh))
    both, over_h, over_y = send_near(1, 1), send_near(0, 1), send_near(1, 0)
    nears = [over_y, over_h, both]
    up1, down1, index, *nears = lax.optimization_barrier((up1, down1, index, *nears))
    left2 = call_join([left0] + nears)
    up2, down2 = z_send(up1, 1), z_send(down1, -1)
    x_send = lambda v, d: lax.ppermute(v, "col", x_perm(d))
    third_x, first_x, second_x = x_send(left2, 3), x_send(left2, 1), x_send(left2, 2)
    lefts = [left2, first_x, second_x, third_x]
    up3, down3 = z_send(up2, 1), z_send(down2, -1)
    near_z = (0, -1, 1, -2, 2)
    rights = call_unpack_right(near_z, index, (right0, up1, down1, up2, down2))
    ready = [(near_z, rights)]
    third = [(-3, (up3,)), (3, (down3,))]
    half = SLABS * BLK // 2
    far = z_send(up3[:half], 1), z_send(down3[half:], -1)

    left = call_unpack_left(False, index, lefts)
    swap = [(0, 1), (1, 0)]
    total = call_multiply(index, left, ready, third)
    give = call_finish(4, False, index, left, far, total)
    recv = lax.ppermute(give, "layer", swap)
    keep = call_finish(4, True, index, left, far, total)
    send = keep + recv
    other = lax.ppermute(send, "row", pair)
    index, send = lax.optimization_barrier((index, send))
    own = call_unpack_left(True, index, lefts)
    mine = call_multiply(index, own, ready, third + [(4, far)])
    theirs = lax.ppermute(mine, "layer", swap)
    rest = lax.ppermute(other, "layer", swap)
    return call_assemble(mine, theirs, other, rest)


def solution(mesh):
    placed = (P("row", ("layer", "col")), P(("layer", "row"), "col"), P(), P())
    return jax.shard_map(
        local, mesh=mesh, in_specs=placed, out_specs=P("row", "col"), check_vma=False
    )
```
